32 devices in a mesh: dp: 4 (over y, x), ctx: 8 (over z, core).
Axes of the slice: x: 2, y: 2, z: 4, core: 2. Of those that a mesh axis runs over, the one named last changes fastest.
Arguments:
- tokens: bfloat16 [8192, 576], P(('dp', 'ctx')), may hold values from -6 to 6
- segment_ids: int32 [8192], P(('dp', 'ctx')), may hold values from 0 to 2, as said below
- positions: int32 [8192], P(('dp', 'ctx')), may hold values from 0 to 6143, as said below
- norm_gains: bfloat16 [2, 576], P(None, 'ctx'), may hold values from 0.099609375 to 1.8984375
- w_query: bfloat16 [576, 576], P('ctx', 'dp'), may hold values from -0.25 to 0.25
- w_key: bfloat16 [576, 192], P('ctx', 'dp'), may hold values from -0.25 to 0.25
- w_value: bfloat16 [576, 192], P('ctx', 'dp'), may hold values from -0.25 to 0.25
- w_out: bfloat16 [576, 576], P('ctx', 'dp'), may hold values from -6 to 6
- w_gate: bfloat16 [576, 1536], P('ctx', 'dp'), may hold values from -0.25 to 0.25
- w_up: bfloat16 [576, 1536], P('ctx', 'dp'), may hold values from -0.25 to 0.25
- w_down: bfloat16 [1536, 576], P('ctx', 'dp'), may hold values from -0.15625 to 0.15625
- cotangent: bfloat16 [8192, 576], P(('dp', 'ctx')), may hold values from -6 to 6
Outputs:
- mixed: bfloat16 [8192, 576], P(('dp', 'ctx'))
- token_grad: float32 [8192, 576], P(('dp', 'ctx'))
- gain_grad: float32 [2, 576], P(None, 'ctx')
- query_grad: float32 [576, 576], P('ctx', 'dp')
- key_grad: float32 [576, 192], P('ctx', 'dp')
- value_grad: float32 [576, 192], P('ctx', 'dp')
- out_grad: float32 [576, 576], P('ctx', 'dp')
- gate_grad: float32 [576, 1536], P('ctx', 'dp')
- up_grad: float32 [576, 1536], P('ctx', 'dp')
- down_grad: float32 [1536, 576], P('ctx', 'dp')
The draws below stay inside these ranges and needn't reach their ends.
Inputs may be any that keep to these rules, and one draw needn't show every extreme that they name: `segment_ids`: in each sequence of 2048 tokens the numbers never fall from token to token; document 1 begins within the first 256 tokens and ends within the last 256. `positions`: within a document the position rises by one from token to token; document 1 begins at position 0; the last token of each sequence has the largest position.
All inputs are finite; a program needn't handle non-finite values.
Results may differ from the reference program's by a relative error of at most 0.015.
Values may be sent and summed in bfloat16 or wider, within the bound.
A program may use at most 128 MiB of HBM per device.

```python
import jax
import jax.numpy as jnp
from jax import lax

D = 576
HEADS = 9
KV_HEADS = 3
HEAD = 64
FF = 1536
TOK_DEV = 256
LENGTH = 2048
TOKENS = 8192
N_DP = 4
N_CTX = 8


def document_bounds(key):
    first_key, last_key, offset_key = jax.random.split(key, 3)
    length = TOK_DEV * N_CTX
    starts = jax.random.randint(first_key, (N_DP, 1), 1, TOK_DEV, dtype=jnp.int32)
    finishes = length - jax.random.randint(last_key, (N_DP, 1), 1, TOK_DEV, dtype=jnp.int32)
    offsets = jax.random.randint(offset_key, (N_DP, 2), 0, 4096, dtype=jnp.int32)
    position_index = jnp.arange(length, dtype=jnp.int32)[None, :]
    numbers = (position_index >= starts).astype(jnp.int32) + (position_index >= finishes).astype(jnp.int32)
    return (position_index, starts, finishes, offsets, numbers)


def draw_segment_ids(key, part):
    position_index, starts, finishes, offsets, numbers = document_bounds(key)
    return numbers.reshape(-1).astype(jnp.int32)


def draw_positions(key, part):
    position_index, starts, finishes, offsets, numbers = document_bounds(key)
    tail_offset = finishes + 4096
    within = jnp.where(numbers == 0, position_index + offsets[:, 0:1], jnp.where(numbers == 1, position_index - starts, position_index - finishes + tail_offset))
    return within.reshape(-1).astype(jnp.int32)


def levels(rng, dims, cuts, smallest, high):
    loudness = 1.0
    for position, parts in cuts:
        heights = jax.random.uniform(jax.random.fold_in(jax.random.fold_in(rng, 6), position), (parts,), jnp.float32, smallest / len(cuts), high / len(cuts))
        loudness = loudness * jnp.repeat(jnp.exp(heights), dims[position] // parts).reshape((-1,) + (1,) * (len(dims) - 1 - position))
    return loudness


def scatter_about(stream_key, dims, scale, reach, shards=(), kind=jnp.bfloat16):
    factor_of = levels(stream_key, dims, shards, -0.22, 0.18) if shards else 1.0
    result = jax.random.normal(stream_key, dims, jnp.float32) * scale * factor_of
    return jnp.minimum(jnp.maximum(result, -reach), reach).astype(kind)


def setup_inputs(seed: int = 0) -> dict:
    splits = jax.random.split(jax.random.key(seed), 13)
    return {
        "tokens": scatter_about(splits[0], (TOKENS, D), 1.0, 6.0, ((0, 32),)),
        "segment_ids": draw_segment_ids(jax.random.fold_in(splits[12], 71), 0),
        "positions": draw_positions(jax.random.fold_in(splits[12], 71), 0),
        "norm_gains": jnp.clip(1.0 + 0.18 * jax.random.normal(splits[3], (2, D), jnp.float32), 0.099609375, 1.8984375).astype(jnp.bfloat16),
        "w_query": scatter_about(splits[4], (D, HEADS * HEAD), D ** -0.5, 0.25, ((0, 8), (1, 4))),
        "w_key": scatter_about(splits[5], (D, KV_HEADS * HEAD), D ** -0.5, 0.25, ((0, 8), (1, 4))),
        "w_value": scatter_about(splits[6], (D, KV_HEADS * HEAD), D ** -0.5, 0.25, ((0, 8), (1, 4))),
        "w_out": scatter_about(splits[7], (HEADS * HEAD, D), (max(1, (TOK_DEV * N_CTX) ** 0.5 // 48)), 6.0, ((0, 8), (1, 4))),
        "w_gate": scatter_about(splits[8], (D, FF), D ** -0.5, 0.25, ((0, 8), (1, 4))),
        "w_up": scatter_about(splits[9], (D, FF), D ** -0.5, 0.25, ((0, 8), (1, 4))),
        "w_down": scatter_about(splits[10], (FF, D), FF ** -0.5, 0.15625, ((0, 8), (1, 4))),
        "cotangent": scatter_about(splits[11], (TOKENS, D), 1.0, 6.0, ((0, 32),)),
    }


EPSILON = 1e-05
ROPE_BASE = 100000.0
MASKED = -1e+30
FULL_PRECISION = lax.Precision.HIGHEST

@jax.custom_vjp
def low(v):
    return lax.optimization_barrier(v.astype(jnp.bfloat16)).astype(jnp.float32)

@jax.custom_vjp
def reduced_backward(v):
    return v

def low_keep(v):
    return (low(v), None)

def low_pass(kept, grad):
    return (grad,)

def back_keep(v):
    return (v, None)

def back_low(kept, grad):
    return (low(grad),)
low.defvjp(low_keep, low_pass)
reduced_backward.defvjp(back_keep, back_low)

def tables(positions):
    half_dim = HEAD // 2
    frequency = ROPE_BASE ** (-(2.0 / HEAD) * jnp.arange(half_dim, dtype=jnp.float32))
    angles = positions.astype(jnp.float32)[:, None] * frequency[None, :]
    return (jnp.cos(angles)[:, None, :], jnp.sin(angles)[:, None, :])

def rotate(values, cosine_table, sine_table):
    half_dim = HEAD // 2
    per_head = values.reshape(values.shape[0], -1, HEAD)
    leading = per_head[..., :half_dim]
    trailing = per_head[..., half_dim:]
    turned = jnp.concatenate([leading * cosine_table - trailing * sine_table, trailing * cosine_table + leading * sine_table], axis=-1)
    return turned.reshape(values.shape)

def rms_norm(hidden, gain_row):
    inverse = lax.rsqrt(lax.optimization_barrier(jnp.mean(hidden * hidden, axis=1, keepdims=True)) + EPSILON)
    return hidden * inverse * gain_row

def sequence_forward(hidden, segments, cosine_table, sine_table, gain_rows, weights):
    w_query, w_key, w_value, w_out, w_gate, w_up, w_down = weights
    repeat = HEADS // KV_HEADS
    length = hidden.shape[0]
    block_rows = min(512, length)
    logit_scale = HEAD ** (-0.5)
    normed_one = low(rms_norm(hidden, gain_rows[0]))
    queries = reduced_backward(jnp.dot(normed_one, w_query, precision=FULL_PRECISION))
    key_proj = reduced_backward(jnp.dot(normed_one, w_key, precision=FULL_PRECISION))
    value_proj = reduced_backward(jnp.dot(normed_one, w_value, precision=FULL_PRECISION))
    queries = low(rotate(queries, cosine_table, sine_table))
    key_proj = low(rotate(key_proj, cosine_table, sine_table))
    value_proj = low(value_proj)
    key_head_rows = key_proj.reshape(length, KV_HEADS, HEAD)
    value_head_rows = value_proj.reshape(length, KV_HEADS, HEAD)
    query_blocks = queries.reshape(length // block_rows, block_rows, KV_HEADS, repeat, HEAD)
    key_index = jnp.arange(length, dtype=jnp.int32)

    def attend(block_args):
        query_block_rows, block_start = block_args
        query_index = block_start + jnp.arange(block_rows, dtype=jnp.int32)
        query_segments = lax.dynamic_slice_in_dim(segments, block_start, block_rows)
        keep_mask = (query_segments[:, None] == segments[None, :]) & (key_index[None, :] <= query_index[:, None])
        attention_scores = reduced_backward(jnp.einsum('xikj,uij->ikxu', query_block_rows, key_head_rows, precision=FULL_PRECISION) * logit_scale)
        attention_scores = jnp.where(keep_mask, attention_scores, MASKED)
        row_top = lax.optimization_barrier(jnp.max(attention_scores, axis=-1, keepdims=True))
        log_total = row_top + jnp.log(lax.optimization_barrier(jnp.sum(jnp.exp(attention_scores - row_top), axis=-1, keepdims=True)))
        reduced_weights = low(jnp.exp(attention_scores - log_total))
        output_block_tile = jnp.einsum('ejfy,yex->fejx', reduced_weights, value_head_rows, precision=FULL_PRECISION)
        return output_block_tile.reshape(block_rows, HEADS * HEAD)
    starts = jnp.arange(length // block_rows, dtype=jnp.int32) * block_rows
    attention_output = lax.map(jax.checkpoint(attend), (query_blocks, starts)).reshape(length, HEADS * HEAD)
    attention = reduced_backward(jnp.dot(low(reduced_backward(attention_output)), w_out, precision=FULL_PRECISION))
    middle = hidden + attention
    normed_two = low(rms_norm(middle, gain_rows[1]))
    gate_out = reduced_backward(jnp.dot(normed_two, w_gate, precision=FULL_PRECISION))
    up_out = reduced_backward(jnp.dot(normed_two, w_up, precision=FULL_PRECISION))
    inner_act = low(jax.nn.silu(gate_out) * up_out)
    return middle + reduced_backward(jnp.dot(inner_act, w_down, precision=FULL_PRECISION))

def reference(tokens, segment_ids, positions, norm_gains, w_query, w_key, w_value, w_out, w_gate, w_up, w_down, cotangent):
    cosine_table, sine_table = tables(positions)
    cosine_table = cosine_table.reshape(N_DP, LENGTH, 1, HEAD // 2)
    sine_table = sine_table.reshape(N_DP, LENGTH, 1, HEAD // 2)
    segments = segment_ids.reshape(N_DP, LENGTH)

    def forward(hidden, gain_rows, q_weight, k_weight, v_weight, o_weight, g_weight, u_weight, d_weight):
        weights = (q_weight, k_weight, v_weight, o_weight, g_weight, u_weight, d_weight)

        def one_sequence(seq_args):
            seq_hidden, seq_segments, seq_cosine, seq_sine = seq_args
            return sequence_forward(seq_hidden, seq_segments, seq_cosine, seq_sine, gain_rows, weights)
        rows_in = hidden.reshape(N_DP, LENGTH, D)
        return lax.map(one_sequence, (rows_in, segments, cosine_table, sine_table)).reshape(TOKENS, D)
    floats = tuple((tensor.astype(jnp.float32) for tensor in (tokens, norm_gains, w_query, w_key, w_value, w_out, w_gate, w_up, w_down)))
    output, pull_back = jax.vjp(forward, *floats)
    gradients = pull_back(cotangent.astype(jnp.float32))
    return (output.astype(jnp.bfloat16), gradients[0], gradients[1], gradients[2], gradients[3], gradients[4], gradients[5], gradients[6], gradients[7], gradients[8])
```

```python
import jax
import jax.numpy as jnp
from jax import lax
from jax.sharding import PartitionSpec as P

HEADS = 9
KV_HEADS = 3
HEAD = 64


EPSILON = 1e-05
ROPE_BASE = 100000.0
MASKED = -1e30


def tables(positions):
    half_dim = HEAD // 2
    frequency = ROPE_BASE ** (-(2.0 / HEAD) * jnp.arange(half_dim, dtype=jnp.float32))
    angles = positions.astype(jnp.float32)[:, None] * frequency[None, :]
    return (jnp.cos(angles)[:, None, :], jnp.sin(angles)[:, None, :])


def rotate(values, cosine_table, sine_table):
    half_dim = HEAD // 2
    per_head = values.reshape(values.shape[0], -1, HEAD)
    leading = per_head[..., :half_dim]
    trailing = per_head[..., half_dim:]
    turned = jnp.concatenate(
        [
            leading * cosine_table - trailing * sine_table,
            trailing * cosine_table + leading * sine_table,
        ],
        axis=-1,
    )
    return turned.reshape(values.shape)


def norm_back(hidden, inverse, gain_row, upstream):
    normed = hidden * inverse
    weighted = gain_row * upstream
    gain_part = jnp.sum(upstream * normed, axis=0)
    input_part = inverse * (weighted - normed * jnp.mean(weighted * normed, axis=1, keepdims=True))
    return (input_part, gain_part)


def gather_weights(shards, gain_rows):
    widened = (
        lax.all_gather(shards[0], "dp", axis=1, tiled=True),
        lax.all_gather(shards[1], "dp", axis=1, tiled=True),
        lax.all_gather(shards[2], "dp", axis=1, tiled=True),
        lax.all_gather(shards[3], "dp", axis=1, tiled=True),
        lax.all_gather(shards[4], "dp", axis=1, tiled=True),
        lax.all_gather(shards[5], "dp", axis=1, tiled=True),
        lax.all_gather(shards[6], "dp", axis=1, tiled=True),
    )
    complete = (
        lax.all_gather(widened[0], "ctx", axis=0, tiled=True),
        lax.all_gather(widened[1], "ctx", axis=0, tiled=True),
        lax.all_gather(widened[2], "ctx", axis=0, tiled=True),
        lax.all_gather(widened[3], "ctx", axis=0, tiled=True),
        lax.all_gather(widened[4], "ctx", axis=0, tiled=True),
        lax.all_gather(widened[5], "ctx", axis=0, tiled=True),
        lax.all_gather(widened[6], "ctx", axis=0, tiled=True),
        lax.all_gather(gain_rows, "ctx", axis=1, tiled=True),
    )
    return (
        (complete[0], complete[1], complete[2], complete[3], complete[4], complete[5], complete[6]),
        complete[7],
    )


def gather_keys(key_values, segments_low):
    return (
        lax.all_gather(key_values, "ctx", axis=0, tiled=True),
        lax.all_gather(segments_low, "ctx", axis=0, tiled=True),
    )


def key_blocks(gathered, rows_here):
    key_values, key_segments = gathered
    length = key_values.shape[0]
    block_width = min(length, 4 * rows_here)
    block_count = length // block_width
    return (
        key_values.reshape(block_count, block_width, key_values.shape[1]),
        key_segments.reshape(block_count, block_width),
        jnp.arange(block_count, dtype=jnp.int32) * block_width,
    )


def block_scores(query_head_rows, block_args, query_segments, query_index, logit_scale):
    key_block, segment_block, block_start = block_args
    block_width = key_block.shape[0]
    key_width = KV_HEADS * HEAD
    key_head_rows = key_block[:, :key_width].reshape(block_width, KV_HEADS, HEAD)
    value_head_rows = key_block[:, key_width:].reshape(block_width, KV_HEADS, HEAD)
    key_index = block_start + jnp.arange(block_width, dtype=jnp.int32)
    keep_mask = (query_segments[:, None] == segment_block[None, :]) & (
        key_index[None, :] <= query_index[:, None]
    )
    raw_scores = (
        jnp.einsum(
            "xikj,uij->ikxu", query_head_rows, key_head_rows, preferred_element_type=jnp.float32
        )
        * logit_scale
    )
    return (raw_scores, keep_mask, key_head_rows, value_head_rows)


def attend_forward(query_head_rows, gathered, query_segments, query_index, logit_scale):
    rows_here = query_head_rows.shape[0]
    blocks = key_blocks(gathered, rows_here)

    def stat_step(carry, block_args):
        row_top, row_total = carry
        raw_scores, keep_mask, key_head_rows, value_head_rows = block_scores(
            query_head_rows, block_args, query_segments, query_index, logit_scale
        )
        masked = jnp.where(keep_mask, raw_scores, MASKED)
        new_top = jnp.maximum(row_top, jnp.max(masked, axis=-1))
        row_total = row_total * jnp.exp(row_top - new_top) + jnp.sum(
            jnp.where(keep_mask, jnp.exp(masked - new_top[..., None]), 0.0), axis=-1
        )
        return ((new_top, row_total), None)

    stat_shape = (KV_HEADS, HEADS // KV_HEADS, rows_here)
    start_carry = (jnp.full(stat_shape, MASKED, jnp.float32), jnp.zeros(stat_shape, jnp.float32))
    (row_top, row_total), unused = lax.scan(stat_step, start_carry, blocks)
    log_total = row_top + jnp.log(row_total)

    def out_step(accumulated, block_args):
        raw_scores, keep_mask, key_head_rows, value_head_rows = block_scores(
            query_head_rows, block_args, query_segments, query_index, logit_scale
        )
        softmax_reduced = jnp.where(
            keep_mask, jnp.exp(raw_scores - log_total[..., None]), 0.0
        ).astype(jnp.bfloat16)
        return (
            accumulated
            + jnp.einsum(
                "ejfy,yex->fejx",
                softmax_reduced,
                value_head_rows,
                preferred_element_type=jnp.float32,
            ),
            None,
        )

    attention_output, unused = lax.scan(
        out_step, jnp.zeros(query_head_rows.shape, jnp.float32), blocks
    )
    return (log_total, attention_output)


def attend_backward(
    query_head_rows,
    gathered,
    query_segments,
    query_index,
    logit_scale,
    log_total,
    attention_output,
    attention_output_grad,
):
    rows_here = query_head_rows.shape[0]
    blocks = key_blocks(gathered, rows_here)
    row_correction = jnp.einsum(
        "qxmv,qxmv->xmq", attention_output_grad.astype(jnp.float32), attention_output
    )

    def back_step(accumulated, block_args):
        raw_scores, keep_mask, key_head_rows, value_head_rows = block_scores(
            query_head_rows, block_args, query_segments, query_index, logit_scale
        )
        probability = jnp.where(keep_mask, jnp.exp(raw_scores - log_total[..., None]), 0.0)
        slopes = jnp.einsum(
            "xikj,uij->ikxu",
            attention_output_grad,
            value_head_rows,
            preferred_element_type=jnp.float32,
        )
        score_gradient = (probability * (slopes - row_correction[..., None])).astype(jnp.bfloat16)
        accumulated = accumulated + jnp.einsum(
            "ejfy,yex->fejx", score_gradient, key_head_rows, preferred_element_type=jnp.float32
        )
        key_part = jnp.einsum(
            "qjif,iqjn->fqn", score_gradient, query_head_rows, preferred_element_type=jnp.float32
        )
        value_part = jnp.einsum(
            "qjif,iqjn->fqn",
            probability.astype(jnp.bfloat16),
            attention_output_grad,
            preferred_element_type=jnp.float32,
        )
        block_width = key_head_rows.shape[0]
        return (
            accumulated,
            jnp.concatenate(
                [key_part.reshape(block_width, -1), value_part.reshape(block_width, -1)], axis=1
            ),
        )

    query_part, stacked = lax.scan(back_step, jnp.zeros(query_head_rows.shape, jnp.float32), blocks)
    return (query_part, stacked.reshape(-1, stacked.shape[-1]))


def body(
    tokens,
    segment_ids,
    positions,
    norm_gains,
    w_query,
    w_key,
    w_value,
    w_out,
    w_gate,
    w_up,
    w_down,
    cotangent,
):
    shards = (w_query, w_key, w_value, w_out, w_gate, w_up, w_down)
    weights, gain_rows = gather_weights(shards, norm_gains)
    repeat = HEADS // KV_HEADS
    key_width = KV_HEADS * HEAD
    logit_scale = HEAD ** (-0.5)
    rows_here = tokens.shape[0]
    query_index = lax.axis_index("ctx") * rows_here + jnp.arange(rows_here, dtype=jnp.int32)
    cosine_table, sine_table = tables(positions)
    hidden = tokens.astype(jnp.float32)
    gain_one = gain_rows[0].astype(jnp.float32)
    gain_two = gain_rows[1].astype(jnp.float32)
    inverse_one = lax.rsqrt(jnp.mean(hidden * hidden, axis=1, keepdims=True) + EPSILON)
    normed_one = (hidden * inverse_one * gain_one).astype(jnp.bfloat16)
    queries = rotate(
        jnp.dot(normed_one, weights[0], preferred_element_type=jnp.float32),
        cosine_table,
        sine_table,
    ).astype(jnp.bfloat16)
    key_proj = rotate(
        jnp.dot(normed_one, weights[1], preferred_element_type=jnp.float32),
        cosine_table,
        sine_table,
    ).astype(jnp.bfloat16)
    value_proj = jnp.dot(normed_one, weights[2], preferred_element_type=jnp.float32).astype(
        jnp.bfloat16
    )
    key_values = jnp.concatenate([key_proj, value_proj], axis=1)
    segments_low = segment_ids.astype(jnp.bfloat16)
    gathered = gather_keys(key_values, segments_low)
    query_head_rows = queries.reshape(rows_here, KV_HEADS, repeat, HEAD)
    log_total, attention_output = attend_forward(
        query_head_rows, gathered, segments_low, query_index, logit_scale
    )
    attended_low = attention_output.reshape(rows_here, HEADS * HEAD).astype(jnp.bfloat16)
    middle = hidden + jnp.dot(attended_low, weights[3], preferred_element_type=jnp.float32)
    inverse_two = lax.rsqrt(jnp.mean(middle * middle, axis=1, keepdims=True) + EPSILON)
    normed_two = (middle * inverse_two * gain_two).astype(jnp.bfloat16)
    gate_out = jnp.dot(normed_two, weights[4], preferred_element_type=jnp.float32)
    up_out = jnp.dot(normed_two, weights[5], preferred_element_type=jnp.float32)
    inner_act = (jax.nn.silu(gate_out) * up_out).astype(jnp.bfloat16)
    mixed_out = (
        middle + jnp.dot(inner_act, weights[6], preferred_element_type=jnp.float32)
    ).astype(jnp.bfloat16)
    weights, gain_rows = gather_weights(shards, norm_gains)
    gathered = gather_keys(key_values, segments_low)
    down_weight_grad = jnp.einsum(
        "tf,td->fd", inner_act, cotangent, preferred_element_type=jnp.float32
    )
    inner_grad = jnp.einsum("td,fd->tf", cotangent, weights[6], preferred_element_type=jnp.float32)
    sigmoid_gate = jax.nn.sigmoid(gate_out)
    silu_gate = gate_out * sigmoid_gate
    gate_grad_low = (
        inner_grad * up_out * sigmoid_gate * (1.0 + gate_out * (1.0 - sigmoid_gate))
    ).astype(jnp.bfloat16)
    up_grad_low = (inner_grad * silu_gate).astype(jnp.bfloat16)
    gate_weight_grad = jnp.einsum(
        "td,tf->df", normed_two, gate_grad_low, preferred_element_type=jnp.float32
    )
    up_weight_grad = jnp.einsum(
        "td,tf->df", normed_two, up_grad_low, preferred_element_type=jnp.float32
    )
    normed_two_grad = jnp.einsum(
        "tf,df->td", gate_grad_low, weights[4], preferred_element_type=jnp.float32
    )
    normed_two_grad = normed_two_grad + jnp.einsum(
        "tf,df->td", up_grad_low, weights[5], preferred_element_type=jnp.float32
    )
    middle_grad, gain_two_grad = norm_back(middle, inverse_two, gain_two, normed_two_grad)
    middle_grad = middle_grad + cotangent.astype(jnp.float32)
    branch_low = middle_grad.astype(jnp.bfloat16)
    out_weight_grad = jnp.einsum(
        "tc,td->cd", attended_low, branch_low, preferred_element_type=jnp.float32
    )
    attention_output_grad = jnp.einsum(
        "td,cd->tc", branch_low, weights[3], preferred_element_type=jnp.float32
    ).astype(jnp.bfloat16)
    query_part, key_value_part = attend_backward(
        query_head_rows,
        gathered,
        segments_low,
        query_index,
        logit_scale,
        log_total,
        attention_output,
        attention_output_grad.reshape(rows_here, KV_HEADS, repeat, HEAD),
    )
    own_grads = lax.psum_scatter(key_value_part, "ctx", scatter_dimension=0, tiled=True)
    query_low = rotate(
        query_part.reshape(rows_here, HEADS * HEAD) * logit_scale, cosine_table, -sine_table
    ).astype(jnp.bfloat16)
    key_low = rotate(own_grads[:, :key_width] * logit_scale, cosine_table, -sine_table).astype(
        jnp.bfloat16
    )
    value_low = own_grads[:, key_width:].astype(jnp.bfloat16)
    query_weight_grad = jnp.einsum(
        "td,tc->dc", normed_one, query_low, preferred_element_type=jnp.float32
    )
    key_weight_grad = jnp.einsum(
        "td,tc->dc", normed_one, key_low, preferred_element_type=jnp.float32
    )
    value_weight_grad = jnp.einsum(
        "td,tc->dc", normed_one, value_low, preferred_element_type=jnp.float32
    )
    normed_one_grad = jnp.einsum(
        "tc,dc->td", query_low, weights[0], preferred_element_type=jnp.float32
    )
    normed_one_grad = normed_one_grad + jnp.einsum(
        "tc,dc->td", key_low, weights[1], preferred_element_type=jnp.float32
    )
    normed_one_grad = normed_one_grad + jnp.einsum(
        "tc,dc->td", value_low, weights[2], preferred_element_type=jnp.float32
    )
    hidden_grad, gain_one_grad = norm_back(hidden, inverse_one, gain_one, normed_one_grad)
    token_grad = middle_grad + hidden_grad
    gain_terms = jnp.stack([gain_one_grad, gain_two_grad])
    reduced = (
        lax.psum_scatter(query_weight_grad, "ctx", scatter_dimension=0, tiled=True),
        lax.psum_scatter(key_weight_grad, "ctx", scatter_dimension=0, tiled=True),
        lax.psum_scatter(value_weight_grad, "ctx", scatter_dimension=0, tiled=True),
        lax.psum_scatter(out_weight_grad, "ctx", scatter_dimension=0, tiled=True),
        lax.psum_scatter(gate_weight_grad, "ctx", scatter_dimension=0, tiled=True),
        lax.psum_scatter(up_weight_grad, "ctx", scatter_dimension=0, tiled=True),
        lax.psum_scatter(down_weight_grad, "ctx", scatter_dimension=0, tiled=True),
        lax.psum_scatter(gain_terms, "ctx", scatter_dimension=1, tiled=True),
    )
    copies = jnp.tile(reduced[7], (1, lax.axis_size("dp")))
    owned_grads = (
        lax.psum_scatter(
            reduced[0].astype(jnp.bfloat16), "dp", scatter_dimension=1, tiled=True
        ).astype(jnp.float32),
        lax.psum_scatter(
            reduced[1].astype(jnp.bfloat16), "dp", scatter_dimension=1, tiled=True
        ).astype(jnp.float32),
        lax.psum_scatter(
            reduced[2].astype(jnp.bfloat16), "dp", scatter_dimension=1, tiled=True
        ).astype(jnp.float32),
        lax.psum_scatter(
            reduced[3].astype(jnp.bfloat16), "dp", scatter_dimension=1, tiled=True
        ).astype(jnp.float32),
        lax.psum_scatter(
            reduced[4].astype(jnp.bfloat16), "dp", scatter_dimension=1, tiled=True
        ).astype(jnp.float32),
        lax.psum_scatter(
            reduced[5].astype(jnp.bfloat16), "dp", scatter_dimension=1, tiled=True
        ).astype(jnp.float32),
        lax.psum_scatter(
            reduced[6].astype(jnp.bfloat16), "dp", scatter_dimension=1, tiled=True
        ).astype(jnp.float32),
        lax.psum_scatter(copies.astype(jnp.bfloat16), "dp", scatter_dimension=1, tiled=True).astype(
            jnp.float32
        ),
    )
    return (
        mixed_out,
        token_grad,
        owned_grads[7],
        owned_grads[0],
        owned_grads[1],
        owned_grads[2],
        owned_grads[3],
        owned_grads[4],
        owned_grads[5],
        owned_grads[6],
    )


def z_permute(block, shift, wrap):
    size = lax.axis_size("ctx")
    pairs = [
        (c, (c + 2 * shift) % size)
        for c in range(size)
        if wrap or 0 <= c + 2 * shift < size
    ]
    return lax.ppermute(block, "ctx", pairs)


def core_permute(block):
    return lax.ppermute(block, "ctx", [(c, c ^ 1) for c in range(lax.axis_size("ctx"))])


def dp_permute(block, offset):
    size = lax.axis_size("dp")
    return lax.ppermute(block, "dp", [(d, d ^ offset) for d in range(size)])


def place(pieces, indices):
    stacked = jnp.zeros((len(pieces),) + pieces[0].shape, pieces[0].dtype)
    for piece, index in zip(pieces, indices):
        stacked = lax.dynamic_update_index_in_dim(stacked, piece, index, 0)
    return stacked


def core_pair(mine, other):
    first = lax.axis_index("ctx") % 2 == 0
    return (jnp.where(first, mine, other), jnp.where(first, other, mine))


def spread_gather(block):
    depth = lax.axis_size("ctx") // 2
    level = lax.axis_index("ctx") // 2
    column = lax.axis_index("dp")
    along = place(
        [block] + [z_permute(block, s, True) for s in range(1, depth)],
        [(level - s) % depth for s in range(depth)],
    )
    across = place(
        [along] + [dp_permute(along, s) for s in range(1, lax.axis_size("dp"))],
        [column ^ s for s in range(lax.axis_size("dp"))],
    )
    even, odd = core_pair(across, core_permute(across))
    return jnp.stack([even, odd], axis=2)


def spread_sum(blocks):
    depth = lax.axis_size("ctx") // 2
    level = lax.axis_index("ctx") // 2
    core = lax.axis_index("ctx") % 2
    column = lax.axis_index("dp")
    kept = lax.dynamic_index_in_dim(blocks, core, 2, keepdims=False)
    sent = lax.dynamic_index_in_dim(blocks, 1 - core, 2, keepdims=False)
    half = (kept.astype(jnp.float32) + core_permute(sent).astype(jnp.float32)).astype(jnp.bfloat16)
    total = lax.dynamic_index_in_dim(half, column, 0, keepdims=False).astype(jnp.float32)
    for s in range(1, lax.axis_size("dp")):
        part = lax.dynamic_index_in_dim(half, column ^ s, 0, keepdims=False)
        total = total + dp_permute(part, s).astype(jnp.float32)
    quarter = total.astype(jnp.bfloat16)
    result = lax.dynamic_index_in_dim(quarter, level, 0, keepdims=False).astype(jnp.float32)
    for s in range(1, depth):
        part = lax.dynamic_index_in_dim(quarter, (level + s) % depth, 0, keepdims=False)
        result = result + z_permute(part, s, True).astype(jnp.float32)
    return result


def assemble(gathered, begin, width):
    dp, depth, cores, rows = gathered.shape[:4]
    part = gathered[..., begin : begin + width].reshape(dp, depth * cores * rows, width)
    return jnp.transpose(part, (1, 0, 2)).reshape(depth * cores * rows, dp * width)


def cut(matrix):
    dp, ctx = lax.axis_size("dp"), lax.axis_size("ctx")
    rows, width = matrix.shape[0] // ctx, matrix.shape[1] // dp
    blocks = matrix.astype(jnp.bfloat16).reshape(ctx // 2, 2, rows, dp, width)
    return jnp.transpose(blocks, (3, 0, 1, 2, 4))


def chain_gather(block):
    depth = lax.axis_size("ctx") // 2
    level = lax.axis_index("ctx") // 2
    along = place(
        [block] + [z_permute(block, s, False) for s in range(1, depth)],
        [(level - s) % depth for s in range(depth)],
    )
    even, odd = core_pair(along, core_permute(along))
    return jnp.stack([even, odd], axis=1)


def chain_sum(blocks):
    depth = lax.axis_size("ctx") // 2
    level = lax.axis_index("ctx") // 2
    core = lax.axis_index("ctx") % 2
    kept = lax.dynamic_index_in_dim(blocks, core, 1, keepdims=False)
    sent = lax.dynamic_index_in_dim(blocks, 1 - core, 1, keepdims=False).astype(jnp.bfloat16)
    half = kept + core_permute(sent).astype(jnp.float32)
    result = lax.dynamic_index_in_dim(half, level, 0, keepdims=False)
    for s in range(1, depth):
        part = lax.dynamic_index_in_dim(half, (level - s) % depth, 0, keepdims=False)
        result = result + z_permute(part.astype(jnp.bfloat16), -s, False).astype(jnp.float32)
    return result


def staged_body(
    tokens,
    segment_ids,
    positions,
    norm_gains,
    w_query,
    w_key,
    w_value,
    w_out,
    w_gate,
    w_up,
    w_down,
    cotangent,
):
    first = spread_gather(jnp.concatenate([w_query, w_key, w_value, norm_gains.T], axis=1))
    second = spread_gather(jnp.concatenate([w_out, w_gate, w_up], axis=1))
    third = spread_gather(w_down)
    nq, nk, ng = w_query.shape[1], w_key.shape[1], w_gate.shape[1]
    weights = (
        assemble(first, 0, nq),
        assemble(first, nq, nk),
        assemble(first, nq + nk, nk),
        assemble(second, 0, nq),
        assemble(second, nq, ng),
        assemble(second, nq + ng, ng),
        assemble(third, 0, nq),
    )
    gain_rows = first[0, ..., nq + 2 * nk :].reshape(-1, 2).T
    repeat = HEADS // KV_HEADS
    key_width = KV_HEADS * HEAD
    logit_scale = HEAD ** (-0.5)
    rows_here = tokens.shape[0]
    query_index = lax.axis_index("ctx") * rows_here + jnp.arange(rows_here, dtype=jnp.int32)
    cosine_table, sine_table = tables(positions)
    hidden = tokens.astype(jnp.float32)
    gain_one = gain_rows[0].astype(jnp.float32)
    gain_two = gain_rows[1].astype(jnp.float32)
    inverse_one = lax.rsqrt(jnp.mean(hidden * hidden, axis=1, keepdims=True) + EPSILON)
    normed_one = (hidden * inverse_one * gain_one).astype(jnp.bfloat16)
    queries = rotate(
        jnp.dot(normed_one, weights[0], preferred_element_type=jnp.float32),
        cosine_table,
        sine_table,
    ).astype(jnp.bfloat16)
    key_proj = rotate(
        jnp.dot(normed_one, weights[1], preferred_element_type=jnp.float32),
        cosine_table,
        sine_table,
    ).astype(jnp.bfloat16)
    value_proj = jnp.dot(normed_one, weights[2], preferred_element_type=jnp.float32).astype(
        jnp.bfloat16
    )
    key_values = jnp.concatenate([key_proj, value_proj], axis=1)
    segments_low = segment_ids.astype(jnp.bfloat16)
    spare = jnp.zeros((16, 2 * key_width), jnp.bfloat16)
    spare = spare.at[0, :rows_here].set(segments_low)
    parts = chain_gather(jnp.concatenate([key_values, spare], axis=0))
    gathered = (
        parts[:, :, :rows_here].reshape(-1, 2 * key_width),
        parts[:, :, rows_here, :rows_here].reshape(-1),
    )
    query_head_rows = queries.reshape(rows_here, KV_HEADS, repeat, HEAD)
    log_total, attention_output = attend_forward(
        query_head_rows, gathered, segments_low, query_index, logit_scale
    )
    attended_low = attention_output.reshape(rows_here, HEADS * HEAD).astype(jnp.bfloat16)
    middle = hidden + jnp.dot(attended_low, weights[3], preferred_element_type=jnp.float32)
    inverse_two = lax.rsqrt(jnp.mean(middle * middle, axis=1, keepdims=True) + EPSILON)
    normed_two = (middle * inverse_two * gain_two).astype(jnp.bfloat16)
    gate_out = jnp.dot(normed_two, weights[4], preferred_element_type=jnp.float32)
    up_out = jnp.dot(normed_two, weights[5], preferred_element_type=jnp.float32)
    inner_act = (jax.nn.silu(gate_out) * up_out).astype(jnp.bfloat16)
    mixed_out = (
        middle + jnp.dot(inner_act, weights[6], preferred_element_type=jnp.float32)
    ).astype(jnp.bfloat16)
    down_weight_grad = jnp.einsum(
        "tf,td->fd", inner_act, cotangent, preferred_element_type=jnp.float32
    )
    inner_grad = jnp.einsum("td,fd->tf", cotangent, weights[6], preferred_element_type=jnp.float32)
    sigmoid_gate = jax.nn.sigmoid(gate_out)
    silu_gate = gate_out * sigmoid_gate
    gate_grad_low = (
        inner_grad * up_out * sigmoid_gate * (1.0 + gate_out * (1.0 - sigmoid_gate))
    ).astype(jnp.bfloat16)
    up_grad_low = (inner_grad * silu_gate).astype(jnp.bfloat16)
    gate_weight_grad = jnp.einsum(
        "td,tf->df", normed_two, gate_grad_low, preferred_element_type=jnp.float32
    )
    up_weight_grad = jnp.einsum(
        "td,tf->df", normed_two, up_grad_low, preferred_element_type=jnp.float32
    )
    normed_two_grad = jnp.einsum(
        "tf,df->td", gate_grad_low, weights[4], preferred_element_type=jnp.float32
    )
    normed_two_grad = normed_two_grad + jnp.einsum(
        "tf,df->td", up_grad_low, weights[5], preferred_element_type=jnp.float32
    )
    middle_grad, gain_two_grad = norm_back(middle, inverse_two, gain_two, normed_two_grad)
    middle_grad = middle_grad + cotangent.astype(jnp.float32)
    branch_low = middle_grad.astype(jnp.bfloat16)
    out_weight_grad = jnp.einsum(
        "tc,td->cd", attended_low, branch_low, preferred_element_type=jnp.float32
    )
    attention_output_grad = jnp.einsum(
        "td,cd->tc", branch_low, weights[3], preferred_element_type=jnp.float32
    ).astype(jnp.bfloat16)
    query_part, key_value_part = attend_backward(
        query_head_rows,
        gathered,
        segments_low,
        query_index,
        logit_scale,
        log_total,
        attention_output,
        attention_output_grad.reshape(rows_here, KV_HEADS, repeat, HEAD),
    )
    own_grads = chain_sum(
        key_value_part.reshape(lax.axis_size("ctx") // 2, 2, rows_here, 2 * key_width)
    )
    query_low = rotate(
        query_part.reshape(rows_here, HEADS * HEAD) * logit_scale, cosine_table, -sine_table
    ).astype(jnp.bfloat16)
    key_low = rotate(own_grads[:, :key_width] * logit_scale, cosine_table, -sine_table).astype(
        jnp.bfloat16
    )
    value_low = own_grads[:, key_width:].astype(jnp.bfloat16)
    query_weight_grad = jnp.einsum(
        "td,tc->dc", normed_one, query_low, preferred_element_type=jnp.float32
    )
    key_weight_grad = jnp.einsum(
        "td,tc->dc", normed_one, key_low, preferred_element_type=jnp.float32
    )
    value_weight_grad = jnp.einsum(
        "td,tc->dc", normed_one, value_low, preferred_element_type=jnp.float32
    )
    normed_one_grad = jnp.einsum(
        "tc,dc->td", query_low, weights[0], preferred_element_type=jnp.float32
    )
    normed_one_grad = normed_one_grad + jnp.einsum(
        "tc,dc->td", key_low, weights[1], preferred_element_type=jnp.float32
    )
    normed_one_grad = normed_one_grad + jnp.einsum(
        "tc,dc->td", value_low, weights[2], preferred_element_type=jnp.float32
    )
    hidden_grad, gain_one_grad = norm_back(hidden, inverse_one, gain_one, normed_one_grad)
    token_grad = middle_grad + hidden_grad
    gain_terms = jnp.stack([gain_one_grad, gain_two_grad])
    down_grad = spread_sum(cut(down_weight_grad))
    second_grad = spread_sum(
        jnp.concatenate(
            [cut(out_weight_grad), cut(gate_weight_grad), cut(up_weight_grad)], axis=-1
        )
    )
    gain_blocks = jnp.tile(gain_terms.T, (1, lax.axis_size("dp")))
    first_grad = spread_sum(
        jnp.concatenate(
            [cut(query_weight_grad), cut(key_weight_grad), cut(value_weight_grad), cut(gain_blocks)],
            axis=-1,
        )
    )
    return (
        mixed_out,
        token_grad,
        first_grad[:, nq + 2 * nk :].T,
        first_grad[:, :nq],
        first_grad[:, nq : nq + nk],
        first_grad[:, nq + nk : nq + 2 * nk],
        second_grad[:, :nq],
        second_grad[:, nq : nq + ng],
        second_grad[:, nq + ng :],
        down_grad,
    )


def solution(mesh):
    dp, ctx = mesh.shape["dp"], mesh.shape["ctx"]
    placed = (
        P(("dp", "ctx"), None),
        P(("dp", "ctx")),
        P(("dp", "ctx")),
        P(None, "ctx"),
        P("ctx", "dp"),
        P("ctx", "dp"),
        P("ctx", "dp"),
        P("ctx", "dp"),
        P("ctx", "dp"),
        P("ctx", "dp"),
        P("ctx", "dp"),
        P(("dp", "ctx"), None),
    )
    return jax.shard_map(
        staged_body if dp == 4 and ctx == 8 else body,
        mesh=mesh,
        in_specs=placed,
        out_specs=(
            P(("dp", "ctx"), None),
            P(("dp", "ctx"), None),
            P(None, "ctx"),
            P("ctx", "dp"),
            P("ctx", "dp"),
            P("ctx", "dp"),
            P("ctx", "dp"),
            P("ctx", "dp"),
            P("ctx", "dp"),
            P("ctx", "dp"),
        ),
        check_vma=False,
    )
```

```python
import jax
import jax.numpy as jnp
from jax import lax
from jax.experimental import pallas as pl
from jax.experimental.pallas import tpu as pltpu
from jax.sharding import PartitionSpec as P

HEADS = 9
KV_HEADS = 3
HEAD = 64


EPSILON = 1e-05
ROPE_BASE = 100000.0
MASKED = -1e30


def tables(positions):
    half_dim = HEAD // 2
    frequency = ROPE_BASE ** (-(2.0 / HEAD) * jnp.arange(half_dim, dtype=jnp.float32))
    angles = positions.astype(jnp.float32)[:, None] * frequency[None, :]
    return (jnp.cos(angles)[:, None, :], jnp.sin(angles)[:, None, :])


def rotate(values, cosine_table, sine_table):
    half_dim = HEAD // 2
    per_head = values.reshape(values.shape[0], -1, HEAD)
    leading = per_head[..., :half_dim]
    trailing = per_head[..., half_dim:]
    turned = jnp.concatenate(
        [
            leading * cosine_table - trailing * sine_table,
            trailing * cosine_table + leading * sine_table,
        ],
        axis=-1,
    )
    return turned.reshape(values.shape)


def norm_back(hidden, inverse, gain_row, upstream):
    normed = hidden * inverse
    weighted = gain_row * upstream
    gain_part = jnp.sum(upstream * normed, axis=0)
    input_part = inverse * (weighted - normed * jnp.mean(weighted * normed, axis=1, keepdims=True))
    return (input_part, gain_part)


def gather_weights(shards, gain_rows):
    widened = (
        lax.all_gather(shards[0], "dp", axis=1, tiled=True),
        lax.all_gather(shards[1], "dp", axis=1, tiled=True),
        lax.all_gather(shards[2], "dp", axis=1, tiled=True),
        lax.all_gather(shards[3], "dp", axis=1, tiled=True),
        lax.all_gather(shards[4], "dp", axis=1, tiled=True),
        lax.all_gather(shards[5], "dp", axis=1, tiled=True),
        lax.all_gather(shards[6], "dp", axis=1, tiled=True),
    )
    complete = (
        lax.all_gather(widened[0], "ctx", axis=0, tiled=True),
        lax.all_gather(widened[1], "ctx", axis=0, tiled=True),
        lax.all_gather(widened[2], "ctx", axis=0, tiled=True),
        lax.all_gather(widened[3], "ctx", axis=0, tiled=True),
        lax.all_gather(widened[4], "ctx", axis=0, tiled=True),
        lax.all_gather(widened[5], "ctx", axis=0, tiled=True),
        lax.all_gather(widened[6], "ctx", axis=0, tiled=True),
        lax.all_gather(gain_rows, "ctx", axis=1, tiled=True),
    )
    return (
        (complete[0], complete[1], complete[2], complete[3], complete[4], complete[5], complete[6]),
        complete[7],
    )


def gather_keys(key_values, segments_low):
    return (
        lax.all_gather(key_values, "ctx", axis=0, tiled=True),
        lax.all_gather(segments_low, "ctx", axis=0, tiled=True),
    )


def key_blocks(gathered, rows_here):
    key_values, key_segments = gathered
    length = key_values.shape[0]
    block_width = min(length, 4 * rows_here)
    block_count = length // block_width
    return (
        key_values.reshape(block_count, block_width, key_values.shape[1]),
        key_segments.reshape(block_count, block_width),
        jnp.arange(block_count, dtype=jnp.int32) * block_width,
    )


def block_scores(query_head_rows, block_args, query_segments, query_index, logit_scale):
    key_block, segment_block, block_start = block_args
    block_width = key_block.shape[0]
    key_width = KV_HEADS * HEAD
    key_head_rows = key_block[:, :key_width].reshape(block_width, KV_HEADS, HEAD)
    value_head_rows = key_block[:, key_width:].reshape(block_width, KV_HEADS, HEAD)
    key_index = block_start + jnp.arange(block_width, dtype=jnp.int32)
    keep_mask = (query_segments[:, None] == segment_block[None, :]) & (
        key_index[None, :] <= query_index[:, None]
    )
    raw_scores = (
        jnp.einsum(
            "xikj,uij->ikxu", query_head_rows, key_head_rows, preferred_element_type=jnp.float32
        )
        * logit_scale
    )
    return (raw_scores, keep_mask, key_head_rows, value_head_rows)


def attend_forward(query_head_rows, gathered, query_segments, query_index, logit_scale):
    rows_here = query_head_rows.shape[0]
    blocks = key_blocks(gathered, rows_here)

    def stat_step(carry, block_args):
        row_top, row_total = carry
        raw_scores, keep_mask, key_head_rows, value_head_rows = block_scores(
            query_head_rows, block_args, query_segments, query_index, logit_scale
        )
        masked = jnp.where(keep_mask, raw_scores, MASKED)
        new_top = jnp.maximum(row_top, jnp.max(masked, axis=-1))
        row_total = row_total * jnp.exp(row_top - new_top) + jnp.sum(
            jnp.where(keep_mask, jnp.exp(masked - new_top[..., None]), 0.0), axis=-1
        )
        return ((new_top, row_total), None)

    stat_shape = (KV_HEADS, HEADS // KV_HEADS, rows_here)
    start_carry = (jnp.full(stat_shape, MASKED, jnp.float32), jnp.zeros(stat_shape, jnp.float32))
    (row_top, row_total), unused = lax.scan(stat_step, start_carry, blocks)
    log_total = row_top + jnp.log(row_total)

    def out_step(accumulated, block_args):
        raw_scores, keep_mask, key_head_rows, value_head_rows = block_scores(
            query_head_rows, block_args, query_segments, query_index, logit_scale
        )
        softmax_reduced = jnp.where(
            keep_mask, jnp.exp(raw_scores - log_total[..., None]), 0.0
        ).astype(jnp.bfloat16)
        return (
            accumulated
            + jnp.einsum(
                "ejfy,yex->fejx",
                softmax_reduced,
                value_head_rows,
                preferred_element_type=jnp.float32,
            ),
            None,
        )

    attention_output, unused = lax.scan(
        out_step, jnp.zeros(query_head_rows.shape, jnp.float32), blocks
    )
    return (log_total, attention_output)


def attend_backward(
    query_head_rows,
    gathered,
    query_segments,
    query_index,
    logit_scale,
    log_total,
    attention_output,
    attention_output_grad,
):
    rows_here = query_head_rows.shape[0]
    blocks = key_blocks(gathered, rows_here)
    row_correction = jnp.einsum(
        "qxmv,qxmv->xmq", attention_output_grad.astype(jnp.float32), attention_output
    )

    def back_step(accumulated, block_args):
        raw_scores, keep_mask, key_head_rows, value_head_rows = block_scores(
            query_head_rows, block_args, query_segments, query_index, logit_scale
        )
        probability = jnp.where(keep_mask, jnp.exp(raw_scores - log_total[..., None]), 0.0)
        slopes = jnp.einsum(
            "xikj,uij->ikxu",
            attention_output_grad,
            value_head_rows,
            preferred_element_type=jnp.float32,
        )
        score_gradient = (probability * (slopes - row_correction[..., None])).astype(jnp.bfloat16)
        accumulated = accumulated + jnp.einsum(
            "ejfy,yex->fejx", score_gradient, key_head_rows, preferred_element_type=jnp.float32
        )
        key_part = jnp.einsum(
            "qjif,iqjn->fqn", score_gradient, query_head_rows, preferred_element_type=jnp.float32
        )
        value_part = jnp.einsum(
            "qjif,iqjn->fqn",
            probability.astype(jnp.bfloat16),
            attention_output_grad,
            preferred_element_type=jnp.float32,
        )
        block_width = key_head_rows.shape[0]
        return (
            accumulated,
            jnp.concatenate(
                [key_part.reshape(block_width, -1), value_part.reshape(block_width, -1)], axis=1
            ),
        )

    query_part, stacked = lax.scan(back_step, jnp.zeros(query_head_rows.shape, jnp.float32), blocks)
    return (query_part, stacked.reshape(-1, stacked.shape[-1]))


def body(
    tokens,
    segment_ids,
    positions,
    norm_gains,
    w_query,
    w_key,
    w_value,
    w_out,
    w_gate,
    w_up,
    w_down,
    cotangent,
):
    shards = (w_query, w_key, w_value, w_out, w_gate, w_up, w_down)
    weights, gain_rows = gather_weights(shards, norm_gains)
    repeat = HEADS // KV_HEADS
    key_width = KV_HEADS * HEAD
    logit_scale = HEAD ** (-0.5)
    rows_here = tokens.shape[0]
    query_index = lax.axis_index("ctx") * rows_here + jnp.arange(rows_here, dtype=jnp.int32)
    cosine_table, sine_table = tables(positions)
    hidden = tokens.astype(jnp.float32)
    gain_one = gain_rows[0].astype(jnp.float32)
    gain_two = gain_rows[1].astype(jnp.float32)
    inverse_one = lax.rsqrt(jnp.mean(hidden * hidden, axis=1, keepdims=True) + EPSILON)
    normed_one = (hidden * inverse_one * gain_one).astype(jnp.bfloat16)
    queries = rotate(
        jnp.dot(normed_one, weights[0], preferred_element_type=jnp.float32),
        cosine_table,
        sine_table,
    ).astype(jnp.bfloat16)
    key_proj = rotate(
        jnp.dot(normed_one, weights[1], preferred_element_type=jnp.float32),
        cosine_table,
        sine_table,
    ).astype(jnp.bfloat16)
    value_proj = jnp.dot(normed_one, weights[2], preferred_element_type=jnp.float32).astype(
        jnp.bfloat16
    )
    key_values = jnp.concatenate([key_proj, value_proj], axis=1)
    segments_low = segment_ids.astype(jnp.bfloat16)
    gathered = gather_keys(key_values, segments_low)
    query_head_rows = queries.reshape(rows_here, KV_HEADS, repeat, HEAD)
    log_total, attention_output = attend_forward(
        query_head_rows, gathered, segments_low, query_index, logit_scale
    )
    attended_low = attention_output.reshape(rows_here, HEADS * HEAD).astype(jnp.bfloat16)
    middle = hidden + jnp.dot(attended_low, weights[3], preferred_element_type=jnp.float32)
    inverse_two = lax.rsqrt(jnp.mean(middle * middle, axis=1, keepdims=True) + EPSILON)
    normed_two = (middle * inverse_two * gain_two).astype(jnp.bfloat16)
    gate_out = jnp.dot(normed_two, weights[4], preferred_element_type=jnp.float32)
    up_out = jnp.dot(normed_two, weights[5], preferred_element_type=jnp.float32)
    inner_act = (jax.nn.silu(gate_out) * up_out).astype(jnp.bfloat16)
    mixed_out = (
        middle + jnp.dot(inner_act, weights[6], preferred_element_type=jnp.float32)
    ).astype(jnp.bfloat16)
    weights, gain_rows = gather_weights(shards, norm_gains)
    gathered = gather_keys(key_values, segments_low)
    down_weight_grad = jnp.einsum(
        "tf,td->fd", inner_act, cotangent, preferred_element_type=jnp.float32
    )
    inner_grad = jnp.einsum("td,fd->tf", cotangent, weights[6], preferred_element_type=jnp.float32)
    sigmoid_gate = jax.nn.sigmoid(gate_out)
    silu_gate = gate_out * sigmoid_gate
    gate_grad_low = (
        inner_grad * up_out * sigmoid_gate * (1.0 + gate_out * (1.0 - sigmoid_gate))
    ).astype(jnp.bfloat16)
    up_grad_low = (inner_grad * silu_gate).astype(jnp.bfloat16)
    gate_weight_grad = jnp.einsum(
        "td,tf->df", normed_two, gate_grad_low, preferred_element_type=jnp.float32
    )
    up_weight_grad = jnp.einsum(
        "td,tf->df", normed_two, up_grad_low, preferred_element_type=jnp.float32
    )
    normed_two_grad = jnp.einsum(
        "tf,df->td", gate_grad_low, weights[4], preferred_element_type=jnp.float32
    )
    normed_two_grad = normed_two_grad + jnp.einsum(
        "tf,df->td", up_grad_low, weights[5], preferred_element_type=jnp.float32
    )
    middle_grad, gain_two_grad = norm_back(middle, inverse_two, gain_two, normed_two_grad)
    middle_grad = middle_grad + cotangent.astype(jnp.float32)
    branch_low = middle_grad.astype(jnp.bfloat16)
    out_weight_grad = jnp.einsum(
        "tc,td->cd", attended_low, branch_low, preferred_element_type=jnp.float32
    )
    attention_output_grad = jnp.einsum(
        "td,cd->tc", branch_low, weights[3], preferred_element_type=jnp.float32
    ).astype(jnp.bfloat16)
    query_part, key_value_part = attend_backward(
        query_head_rows,
        gathered,
        segments_low,
        query_index,
        logit_scale,
        log_total,
        attention_output,
        attention_output_grad.reshape(rows_here, KV_HEADS, repeat, HEAD),
    )
    own_grads = lax.psum_scatter(key_value_part, "ctx", scatter_dimension=0, tiled=True)
    query_low = rotate(
        query_part.reshape(rows_here, HEADS * HEAD) * logit_scale, cosine_table, -sine_table
    ).astype(jnp.bfloat16)
    key_low = rotate(own_grads[:, :key_width] * logit_scale, cosine_table, -sine_table).astype(
        jnp.bfloat16
    )
    value_low = own_grads[:, key_width:].astype(jnp.bfloat16)
    query_weight_grad = jnp.einsum(
        "td,tc->dc", normed_one, query_low, preferred_element_type=jnp.float32
    )
    key_weight_grad = jnp.einsum(
        "td,tc->dc", normed_one, key_low, preferred_element_type=jnp.float32
    )
    value_weight_grad = jnp.einsum(
        "td,tc->dc", normed_one, value_low, preferred_element_type=jnp.float32
    )
    normed_one_grad = jnp.einsum(
        "tc,dc->td", query_low, weights[0], preferred_element_type=jnp.float32
    )
    normed_one_grad = normed_one_grad + jnp.einsum(
        "tc,dc->td", key_low, weights[1], preferred_element_type=jnp.float32
    )
    normed_one_grad = normed_one_grad + jnp.einsum(
        "tc,dc->td", value_low, weights[2], preferred_element_type=jnp.float32
    )
    hidden_grad, gain_one_grad = norm_back(hidden, inverse_one, gain_one, normed_one_grad)
    token_grad = middle_grad + hidden_grad
    gain_terms = jnp.stack([gain_one_grad, gain_two_grad])
    reduced = (
        lax.psum_scatter(query_weight_grad, "ctx", scatter_dimension=0, tiled=True),
        lax.psum_scatter(key_weight_grad, "ctx", scatter_dimension=0, tiled=True),
        lax.psum_scatter(value_weight_grad, "ctx", scatter_dimension=0, tiled=True),
        lax.psum_scatter(out_weight_grad, "ctx", scatter_dimension=0, tiled=True),
        lax.psum_scatter(gate_weight_grad, "ctx", scatter_dimension=0, tiled=True),
        lax.psum_scatter(up_weight_grad, "ctx", scatter_dimension=0, tiled=True),
        lax.psum_scatter(down_weight_grad, "ctx", scatter_dimension=0, tiled=True),
        lax.psum_scatter(gain_terms, "ctx", scatter_dimension=1, tiled=True),
    )
    copies = jnp.tile(reduced[7], (1, lax.axis_size("dp")))
    owned_grads = (
        lax.psum_scatter(
            reduced[0].astype(jnp.bfloat16), "dp", scatter_dimension=1, tiled=True
        ).astype(jnp.float32),
        lax.psum_scatter(
            reduced[1].astype(jnp.bfloat16), "dp", scatter_dimension=1, tiled=True
        ).astype(jnp.float32),
        lax.psum_scatter(
            reduced[2].astype(jnp.bfloat16), "dp", scatter_dimension=1, tiled=True
        ).astype(jnp.float32),
        lax.psum_scatter(
            reduced[3].astype(jnp.bfloat16), "dp", scatter_dimension=1, tiled=True
        ).astype(jnp.float32),
        lax.psum_scatter(
            reduced[4].astype(jnp.bfloat16), "dp", scatter_dimension=1, tiled=True
        ).astype(jnp.float32),
        lax.psum_scatter(
            reduced[5].astype(jnp.bfloat16), "dp", scatter_dimension=1, tiled=True
        ).astype(jnp.float32),
        lax.psum_scatter(
            reduced[6].astype(jnp.bfloat16), "dp", scatter_dimension=1, tiled=True
        ).astype(jnp.float32),
        lax.psum_scatter(copies.astype(jnp.bfloat16), "dp", scatter_dimension=1, tiled=True).astype(
            jnp.float32
        ),
    )
    return (
        mixed_out,
        token_grad,
        owned_grads[7],
        owned_grads[0],
        owned_grads[1],
        owned_grads[2],
        owned_grads[3],
        owned_grads[4],
        owned_grads[5],
        owned_grads[6],
    )


def z_permute(block, shift, wrap):
    size = lax.axis_size("ctx")
    pairs = [
        (c, (c + 2 * shift) % size)
        for c in range(size)
        if wrap or 0 <= c + 2 * shift < size
    ]
    return lax.ppermute(block, "ctx", pairs)


def core_permute(block):
    return lax.ppermute(block, "ctx", [(c, c ^ 1) for c in range(lax.axis_size("ctx"))])


def dp_permute(block, offset):
    size = lax.axis_size("dp")
    return lax.ppermute(block, "dp", [(d, d ^ offset) for d in range(size)])


def place(pieces, indices):
    stacked = jnp.zeros((len(pieces),) + pieces[0].shape, pieces[0].dtype)
    for piece, index in zip(pieces, indices):
        stacked = lax.dynamic_update_index_in_dim(stacked, piece, index, 0)
    return stacked


def core_pair(mine, other):
    first = lax.axis_index("ctx") % 2 == 0
    return (jnp.where(first, mine, other), jnp.where(first, other, mine))


def gather_z(block):
    depth = lax.axis_size("ctx") // 2
    level = lax.axis_index("ctx") // 2
    return place(
        [block] + [z_permute(block, s, True) for s in range(1, depth)],
        [(level - s) % depth for s in range(depth)],
    )


def gather_dp(along):
    column = lax.axis_index("dp")
    size = lax.axis_size("dp")
    return place(
        [along] + [dp_permute(along, s) for s in range(1, size)],
        [column ^ s for s in range(size)],
    )


def gather_core(across):
    even, odd = core_pair(across, core_permute(across))
    both = jnp.stack([even, odd], axis=2)
    dp, depth, cores, rows, width = both.shape
    return both.reshape(dp, depth * cores * rows, width)


def sum_core(blocks):
    depth = lax.axis_size("ctx") // 2
    core = lax.axis_index("ctx") % 2
    dp, rows, width = blocks.shape
    blocks = blocks.reshape(dp, depth, 2, rows // (2 * depth), width)
    kept = lax.dynamic_index_in_dim(blocks, core, 2, keepdims=False)
    sent = lax.dynamic_index_in_dim(blocks, 1 - core, 2, keepdims=False)
    return (kept.astype(jnp.float32) + core_permute(sent).astype(jnp.float32)).astype(jnp.bfloat16)


def sum_dp(half):
    column = lax.axis_index("dp")
    total = lax.dynamic_index_in_dim(half, column, 0, keepdims=False).astype(jnp.float32)
    for s in range(1, lax.axis_size("dp")):
        part = lax.dynamic_index_in_dim(half, column ^ s, 0, keepdims=False)
        total = total + dp_permute(part, s).astype(jnp.float32)
    return total.astype(jnp.bfloat16)


def sum_z(quarter):
    depth = lax.axis_size("ctx") // 2
    level = lax.axis_index("ctx") // 2
    result = lax.dynamic_index_in_dim(quarter, level, 0, keepdims=False).astype(jnp.float32)
    for s in range(1, depth):
        part = lax.dynamic_index_in_dim(quarter, (level + s) % depth, 0, keepdims=False)
        result = result + z_permute(part, s, True).astype(jnp.float32)
    return result


def dot_nt(left, right):
    return lax.dot_general(left, right, (((1,), (1,)), ((), ())), preferred_element_type=jnp.float32)


def dot_tn(left, right):
    return lax.dot_general(left, right, (((0,), (0,)), ((), ())), preferred_element_type=jnp.float32)


def dot_nn(left, right):
    return jnp.dot(left, right, preferred_element_type=jnp.float32)


def kept_pairs(row_ref, key_segment_ref):
    rows, length = row_ref.shape[0], key_segment_ref.shape[1]
    key_index = lax.broadcasted_iota(jnp.int32, (rows, length), 1)
    return (row_ref[:, 1:2] == key_segment_ref[...]) & (key_index <= row_ref[:, 0:1])


def forward_kernel(q_ref, kv_ref, row_ref, key_segment_ref, out_ref, lse_ref):
    keep = kept_pairs(row_ref, key_segment_ref)
    outputs = []
    for i in range(HEADS):
        j = i // (HEADS // KV_HEADS)
        key = kv_ref[:, j * HEAD : (j + 1) * HEAD]
        value = kv_ref[:, (KV_HEADS + j) * HEAD : (KV_HEADS + j + 1) * HEAD]
        scores = dot_nt(q_ref[:, i * HEAD : (i + 1) * HEAD], key) * HEAD ** (-0.5)
        scores = jnp.where(keep, scores, MASKED)
        top = jnp.max(scores, axis=1, keepdims=True)
        total = jnp.sum(jnp.exp(scores - top), axis=1, keepdims=True)
        log_total = top + jnp.log(total)
        lse_ref[i] = log_total
        outputs.append(dot_nn(jnp.exp(scores - log_total).astype(jnp.bfloat16), value))
    out_ref[...] = jnp.concatenate(outputs, axis=1)


def backward_kernel(
    q_ref, kv_ref, row_ref, key_segment_ref, lse_ref, out_ref, grad_ref, dq_ref, dkv_ref
):
    keep = kept_pairs(row_ref, key_segment_ref)
    query_parts, key_parts, value_parts = [], [], []
    repeat = HEADS // KV_HEADS
    for j in range(KV_HEADS):
        key = kv_ref[:, j * HEAD : (j + 1) * HEAD]
        value = kv_ref[:, (KV_HEADS + j) * HEAD : (KV_HEADS + j + 1) * HEAD]
        key_part = value_part = None
        for i in range(j * repeat, (j + 1) * repeat):
            query = q_ref[:, i * HEAD : (i + 1) * HEAD]
            grad = grad_ref[:, i * HEAD : (i + 1) * HEAD]
            out = out_ref[:, i * HEAD : (i + 1) * HEAD]
            delta = jnp.sum(grad.astype(jnp.float32) * out, axis=1, keepdims=True)
            scores = jnp.where(keep, dot_nt(query, key) * HEAD ** (-0.5), MASKED)
            weight = jnp.exp(scores - lse_ref[i])
            slope = (weight * (dot_nt(grad, value) - delta)).astype(jnp.bfloat16)
            query_parts.append(dot_nn(slope, key))
            dk = dot_tn(slope, query)
            dv = dot_tn(weight.astype(jnp.bfloat16), grad)
            key_part = dk if key_part is None else key_part + dk
            value_part = dv if value_part is None else value_part + dv
        key_parts.append(key_part)
        value_parts.append(value_part)
    dq_ref[...] = jnp.concatenate(query_parts, axis=1)
    dkv_ref[...] = jnp.concatenate(key_parts + value_parts, axis=1)


def run_kernel(kernel, operands, shapes, flops):
    return pl.pallas_call(
        kernel,
        out_shape=[jax.ShapeDtypeStruct(shape, jnp.float32) for shape in shapes],
        in_specs=[pl.BlockSpec(memory_space=pltpu.VMEM)] * len(operands),
        out_specs=[pl.BlockSpec(memory_space=pltpu.VMEM)] * len(shapes),
        compiler_params=pltpu.CompilerParams(vmem_limit_bytes=48 * 1024 * 1024),
        cost_estimate=pl.CostEstimate(
            flops=flops, bytes_accessed=8 * 1024 * 1024, transcendentals=10 * 1024 * 1024
        ),
    )(*operands)


def chain_gather(block):
    depth = lax.axis_size("ctx") // 2
    level = lax.axis_index("ctx") // 2
    along = place(
        [block] + [z_permute(block, s, False) for s in range(1, depth)],
        [(level - s) % depth for s in range(depth)],
    )
    even, odd = core_pair(along, core_permute(along))
    return jnp.stack([even, odd], axis=1)


def chain_sum(blocks):
    depth = lax.axis_size("ctx") // 2
    level = lax.axis_index("ctx") // 2
    core = lax.axis_index("ctx") % 2
    kept = lax.dynamic_index_in_dim(blocks, core, 1, keepdims=False)
    sent = lax.dynamic_index_in_dim(blocks, 1 - core, 1, keepdims=False).astype(jnp.bfloat16)
    half = kept + core_permute(sent).astype(jnp.float32)
    result = lax.dynamic_index_in_dim(half, level, 0, keepdims=False)
    for s in range(1, depth):
        part = lax.dynamic_index_in_dim(half, (level - s) % depth, 0, keepdims=False)
        result = result + z_permute(part.astype(jnp.bfloat16), -s, False).astype(jnp.float32)
    return result


def staged_body(
    tokens,
    segment_ids,
    positions,
    norm_gains,
    w_query,
    w_key,
    w_value,
    w_out,
    w_gate,
    w_up,
    w_down,
    cotangent,
):
    f32, bf16 = jnp.float32, jnp.bfloat16
    nq, nk, ng = w_query.shape[1], w_key.shape[1], w_gate.shape[1]
    dp = lax.axis_size("dp")
    ctx = lax.axis_size("ctx")
    rows = tokens.shape[0]
    key_width = KV_HEADS * HEAD
    logit_scale = HEAD ** (-0.5)
    first = gather_z(jnp.concatenate([w_query, w_key, w_value, norm_gains.T], axis=1))
    early, late = lax.optimization_barrier(
        (first, (jnp.concatenate([w_gate, w_up, w_out], axis=1), w_down))
    )
    first = gather_core(gather_dp(early))
    second, third = gather_z(late[0]), gather_z(late[1])

    def wide(begin, width):
        return jnp.transpose(first[..., begin : begin + width], (1, 0, 2)).reshape(-1, dp * width)

    wq, wk, wv = wide(0, nq), wide(nq, nk), wide(nq + nk, nk)
    gain_rows = first[0, :, nq + 2 * nk :].T.astype(f32)
    gain_one, gain_two = gain_rows[0], gain_rows[1]
    cosine_table, sine_table = tables(positions)
    hidden = tokens.astype(f32)
    inverse_one = lax.rsqrt(jnp.mean(hidden * hidden, axis=1, keepdims=True) + EPSILON)
    normed_one = (hidden * inverse_one * gain_one).astype(bf16)
    key_proj = rotate(dot_nn(normed_one, wk), cosine_table, sine_table).astype(bf16)
    value_proj = dot_nn(normed_one, wv).astype(bf16)
    spare = jnp.zeros((16, 2 * key_width), bf16).at[0, :rows].set(segment_ids.astype(bf16))
    sent = jnp.concatenate([jnp.concatenate([key_proj, value_proj], axis=1), spare], axis=0)
    sent, second, third = lax.optimization_barrier((sent, second, third))
    second, third = gather_dp(second), gather_dp(third)
    queries = rotate(dot_nn(normed_one, wq), cosine_table, sine_table).astype(bf16)
    parts = chain_gather(sent)
    parts, second, third = lax.optimization_barrier((parts, second, third))
    key_values = parts[:, :, :rows].reshape(-1, 2 * key_width)
    key_segments = parts[:, :, rows, :rows].reshape(1, -1).astype(jnp.int32)
    query_index = lax.axis_index("ctx") * rows + jnp.arange(rows, dtype=jnp.int32)
    row_facts = jnp.stack([query_index, segment_ids], axis=1)
    length = key_values.shape[0]
    shared = (queries, key_values, row_facts, key_segments)
    pair_flops = 2 * HEADS * HEAD * rows * length
    attention_output, log_total = run_kernel(
        forward_kernel, shared, [(rows, HEADS * HEAD), (HEADS, rows, 1)], 2 * pair_flops
    )
    second, third = gather_core(second), gather_core(third)
    wg, wo = second[..., : 2 * ng], second[..., 2 * ng :]

    def lanes(blocks):
        return jnp.concatenate([blocks[n] for n in range(dp)], axis=1)

    def apart(matrix):
        width = matrix.shape[1] // dp
        return jnp.stack([matrix[:, n * width : (n + 1) * width] for n in range(dp)])

    def forth(matrix, blocks):
        return jnp.einsum("tk,dkn->dtn", matrix, blocks, preferred_element_type=f32)

    def back(parts_in, blocks):
        return sum(dot_nt(parts_in[n], blocks[n]) for n in range(dp))

    def grads(matrix, parts_in):
        return jnp.stack([dot_tn(matrix, parts_in[n]).astype(bf16) for n in range(dp)])

    attended_low = attention_output.astype(bf16)
    middle = hidden + lanes(forth(attended_low, wo))
    inverse_two = lax.rsqrt(jnp.mean(middle * middle, axis=1, keepdims=True) + EPSILON)
    normed_two = (middle * inverse_two * gain_two).astype(bf16)
    gate_up = forth(normed_two, wg)
    gate_out, up_out = gate_up[..., :ng], gate_up[..., ng:]
    sigmoid_gate = jax.nn.sigmoid(gate_out)
    silu_gate = gate_out * sigmoid_gate
    inner_act = lanes((silu_gate * up_out).astype(bf16))
    mixed_out = (middle + lanes(forth(inner_act, third))).astype(bf16)
    upstream = apart(cotangent)
    down_half = sum_core(grads(inner_act, upstream))
    inner_grad = apart(back(upstream, third))
    gate_low = inner_grad * up_out * sigmoid_gate * (1.0 + gate_out * (1.0 - sigmoid_gate))
    slopes = jnp.concatenate([gate_low.astype(bf16), (inner_grad * silu_gate).astype(bf16)], axis=2)
    gate_half = sum_core(grads(normed_two, slopes))
    middle_grad, gain_two_grad = norm_back(middle, inverse_two, gain_two, back(slopes, wg))
    middle_grad = middle_grad + cotangent.astype(f32)
    branch = apart(middle_grad.astype(bf16))
    attention_grad = back(branch, wo).astype(bf16)
    out_half = sum_core(grads(attended_low, branch))
    attention_grad, down_half, gate_half = lax.optimization_barrier(
        (attention_grad, down_half, gate_half)
    )
    query_part, key_value_part = run_kernel(
        backward_kernel,
        shared + (log_total, attention_output, attention_grad),
        [(rows, HEADS * HEAD), (length, 2 * key_width)],
        5 * pair_flops,
    )
    down_part, gate_part, out_part = sum_dp(down_half), sum_dp(gate_half), sum_dp(out_half)
    own_grads = chain_sum(key_value_part.reshape(ctx // 2, 2, rows, 2 * key_width))
    query_low = rotate(query_part * logit_scale, cosine_table, -sine_table).astype(bf16)
    own_grads, down_part, gate_part, out_part = lax.optimization_barrier(
        (own_grads, down_part, gate_part, out_part)
    )
    key_low = rotate(own_grads[:, :key_width] * logit_scale, cosine_table, -sine_table)
    key_low = key_low.astype(bf16)
    value_low = own_grads[:, key_width:].astype(bf16)
    normed_one_grad = dot_nt(query_low, wq) + dot_nt(key_low, wk) + dot_nt(value_low, wv)
    hidden_grad, gain_one_grad = norm_back(hidden, inverse_one, gain_one, normed_one_grad)
    token_grad = middle_grad + hidden_grad
    gain_terms = jnp.stack([gain_one_grad, gain_two_grad], axis=1).astype(bf16)
    joined = jnp.concatenate([apart(query_low), apart(key_low), apart(value_low)], axis=2)
    gain_blocks = jnp.broadcast_to(gain_terms[None], (dp,) + gain_terms.shape)
    first_grad = jnp.concatenate([grads(normed_one, joined), gain_blocks], axis=2)
    first_grad = sum_z(sum_dp(sum_core(first_grad)))
    down_grad, gate_grad, out_grad = sum_z(down_part), sum_z(gate_part), sum_z(out_part)
    return (
        mixed_out,
        token_grad,
        first_grad[:, nq + 2 * nk :].T,
        first_grad[:, :nq],
        first_grad[:, nq : nq + nk],
        first_grad[:, nq + nk : nq + 2 * nk],
        out_grad,
        gate_grad[:, :ng],
        gate_grad[:, ng:],
        down_grad,
    )


def solution(mesh):
    dp, ctx = mesh.shape["dp"], mesh.shape["ctx"]
    placed = (
        P(("dp", "ctx"), None),
        P(("dp", "ctx")),
        P(("dp", "ctx")),
        P(None, "ctx"),
        P("ctx", "dp"),
        P("ctx", "dp"),
        P("ctx", "dp"),
        P("ctx", "dp"),
        P("ctx", "dp"),
        P("ctx", "dp"),
        P("ctx", "dp"),
        P(("dp", "ctx"), None),
    )
    return jax.shard_map(
        staged_body if dp == 4 and ctx == 8 else body,
        mesh=mesh,
        in_specs=placed,
        out_specs=(
            P(("dp", "ctx"), None),
            P(("dp", "ctx"), None),
            P(None, "ctx"),
            P("ctx", "dp"),
            P("ctx", "dp"),
            P("ctx", "dp"),
            P("ctx", "dp"),
            P("ctx", "dp"),
            P("ctx", "dp"),
            P("ctx", "dp"),
        ),
        check_vma=False,
    )
```

```python
import jax
import jax.numpy as jnp
from jax import lax
from jax.experimental import pallas as pl
from jax.experimental.pallas import tpu as pltpu
from jax.sharding import PartitionSpec as P

HEADS = 9
KV_HEADS = 3
HEAD = 64


EPSILON = 1e-05
ROPE_BASE = 100000.0
MASKED = -1e30


def tables(positions):
    half_dim = HEAD // 2
    frequency = ROPE_BASE ** (-(2.0 / HEAD) * jnp.arange(half_dim, dtype=jnp.float32))
    angles = positions.astype(jnp.float32)[:, None] * frequency[None, :]
    return (jnp.cos(angles)[:, None, :], jnp.sin(angles)[:, None, :])


def rotate(values, cosine_table, sine_table):
    half_dim = HEAD // 2
    per_head = values.reshape(values.shape[0], -1, HEAD)
    leading = per_head[..., :half_dim]
    trailing = per_head[..., half_dim:]
    turned = jnp.concatenate(
        [
            leading * cosine_table - trailing * sine_table,
            trailing * cosine_table + leading * sine_table,
        ],
        axis=-1,
    )
    return turned.reshape(values.shape)


def norm_back(hidden, inverse, gain_row, upstream):
    normed = hidden * inverse
    weighted = gain_row * upstream
    gain_part = jnp.sum(upstream * normed, axis=0)
    input_part = inverse * (weighted - normed * jnp.mean(weighted * normed, axis=1, keepdims=True))
    return (input_part, gain_part)


def gather_weights(shards, gain_rows):
    widened = (
        lax.all_gather(shards[0], "dp", axis=1, tiled=True),
        lax.all_gather(shards[1], "dp", axis=1, tiled=True),
        lax.all_gather(shards[2], "dp", axis=1, tiled=True),
        lax.all_gather(shards[3], "dp", axis=1, tiled=True),
        lax.all_gather(shards[4], "dp", axis=1, tiled=True),
        lax.all_gather(shards[5], "dp", axis=1, tiled=True),
        lax.all_gather(shards[6], "dp", axis=1, tiled=True),
    )
    complete = (
        lax.all_gather(widened[0], "ctx", axis=0, tiled=True),
        lax.all_gather(widened[1], "ctx", axis=0, tiled=True),
        lax.all_gather(widened[2], "ctx", axis=0, tiled=True),
        lax.all_gather(widened[3], "ctx", axis=0, tiled=True),
        lax.all_gather(widened[4], "ctx", axis=0, tiled=True),
        lax.all_gather(widened[5], "ctx", axis=0, tiled=True),
        lax.all_gather(widened[6], "ctx", axis=0, tiled=True),
        lax.all_gather(gain_rows, "ctx", axis=1, tiled=True),
    )
    return (
        (complete[0], complete[1], complete[2], complete[3], complete[4], complete[5], complete[6]),
        complete[7],
    )


def gather_keys(key_values, segments_low):
    return (
        lax.all_gather(key_values, "ctx", axis=0, tiled=True),
        lax.all_gather(segments_low, "ctx", axis=0, tiled=True),
    )


def key_blocks(gathered, rows_here):
    key_values, key_segments = gathered
    length = key_values.shape[0]
    block_width = min(length, 4 * rows_here)
    block_count = length // block_width
    return (
        key_values.reshape(block_count, block_width, key_values.shape[1]),
        key_segments.reshape(block_count, block_width),
        jnp.arange(block_count, dtype=jnp.int32) * block_width,
    )


def block_scores(query_head_rows, block_args, query_segments, query_index, logit_scale):
    key_block, segment_block, block_start = block_args
    block_width = key_block.shape[0]
    key_width = KV_HEADS * HEAD
    key_head_rows = key_block[:, :key_width].reshape(block_width, KV_HEADS, HEAD)
    value_head_rows = key_block[:, key_width:].reshape(block_width, KV_HEADS, HEAD)
    key_index = block_start + jnp.arange(block_width, dtype=jnp.int32)
    keep_mask = (query_segments[:, None] == segment_block[None, :]) & (
        key_index[None, :] <= query_index[:, None]
    )
    raw_scores = (
        jnp.einsum(
            "xikj,uij->ikxu", query_head_rows, key_head_rows, preferred_element_type=jnp.float32
        )
        * logit_scale
    )
    return (raw_scores, keep_mask, key_head_rows, value_head_rows)


def attend_forward(query_head_rows, gathered, query_segments, query_index, logit_scale):
    rows_here = query_head_rows.shape[0]
    blocks = key_blocks(gathered, rows_here)

    def stat_step(carry, block_args):
        row_top, row_total = carry
        raw_scores, keep_mask, key_head_rows, value_head_rows = block_scores(
            query_head_rows, block_args, query_segments, query_index, logit_scale
        )
        masked = jnp.where(keep_mask, raw_scores, MASKED)
        new_top = jnp.maximum(row_top, jnp.max(masked, axis=-1))
        row_total = row_total * jnp.exp(row_top - new_top) + jnp.sum(
            jnp.where(keep_mask, jnp.exp(masked - new_top[..., None]), 0.0), axis=-1
        )
        return ((new_top, row_total), None)

    stat_shape = (KV_HEADS, HEADS // KV_HEADS, rows_here)
    start_carry = (jnp.full(stat_shape, MASKED, jnp.float32), jnp.zeros(stat_shape, jnp.float32))
    (row_top, row_total), unused = lax.scan(stat_step, start_carry, blocks)
    log_total = row_top + jnp.log(row_total)

    def out_step(accumulated, block_args):
        raw_scores, keep_mask, key_head_rows, value_head_rows = block_scores(
            query_head_rows, block_args, query_segments, query_index, logit_scale
        )
        softmax_reduced = jnp.where(
            keep_mask, jnp.exp(raw_scores - log_total[..., None]), 0.0
        ).astype(jnp.bfloat16)
        return (
            accumulated
            + jnp.einsum(
                "ejfy,yex->fejx",
                softmax_reduced,
                value_head_rows,
                preferred_element_type=jnp.float32,
            ),
            None,
        )

    attention_output, unused = lax.scan(
        out_step, jnp.zeros(query_head_rows.shape, jnp.float32), blocks
    )
    return (log_total, attention_output)


def attend_backward(
    query_head_rows,
    gathered,
    query_segments,
    query_index,
    logit_scale,
    log_total,
    attention_output,
    attention_output_grad,
):
    rows_here = query_head_rows.shape[0]
    blocks = key_blocks(gathered, rows_here)
    row_correction = jnp.einsum(
        "qxmv,qxmv->xmq", attention_output_grad.astype(jnp.float32), attention_output
    )

    def back_step(accumulated, block_args):
        raw_scores, keep_mask, key_head_rows, value_head_rows = block_scores(
            query_head_rows, block_args, query_segments, query_index, logit_scale
        )
        probability = jnp.where(keep_mask, jnp.exp(raw_scores - log_total[..., None]), 0.0)
        slopes = jnp.einsum(
            "xikj,uij->ikxu",
            attention_output_grad,
            value_head_rows,
            preferred_element_type=jnp.float32,
        )
        score_gradient = (probability * (slopes - row_correction[..., None])).astype(jnp.bfloat16)
        accumulated = accumulated + jnp.einsum(
            "ejfy,yex->fejx", score_gradient, key_head_rows, preferred_element_type=jnp.float32
        )
        key_part = jnp.einsum(
            "qjif,iqjn->fqn", score_gradient, query_head_rows, preferred_element_type=jnp.float32
        )
        value_part = jnp.einsum(
            "qjif,iqjn->fqn",
            probability.astype(jnp.bfloat16),
            attention_output_grad,
            preferred_element_type=jnp.float32,
        )
        block_width = key_head_rows.shape[0]
        return (
            accumulated,
            jnp.concatenate(
                [key_part.reshape(block_width, -1), value_part.reshape(block_width, -1)], axis=1
            ),
        )

    query_part, stacked = lax.scan(back_step, jnp.zeros(query_head_rows.shape, jnp.float32), blocks)
    return (query_part, stacked.reshape(-1, stacked.shape[-1]))


def body(
    tokens,
    segment_ids,
    positions,
    norm_gains,
    w_query,
    w_key,
    w_value,
    w_out,
    w_gate,
    w_up,
    w_down,
    cotangent,
):
    shards = (w_query, w_key, w_value, w_out, w_gate, w_up, w_down)
    weights, gain_rows = gather_weights(shards, norm_gains)
    repeat = HEADS // KV_HEADS
    key_width = KV_HEADS * HEAD
    logit_scale = HEAD ** (-0.5)
    rows_here = tokens.shape[0]
    query_index = lax.axis_index("ctx") * rows_here + jnp.arange(rows_here, dtype=jnp.int32)
    cosine_table, sine_table = tables(positions)
    hidden = tokens.astype(jnp.float32)
    gain_one = gain_rows[0].astype(jnp.float32)
    gain_two = gain_rows[1].astype(jnp.float32)
    inverse_one = lax.rsqrt(jnp.mean(hidden * hidden, axis=1, keepdims=True) + EPSILON)
    normed_one = (hidden * inverse_one * gain_one).astype(jnp.bfloat16)
    queries = rotate(
        jnp.dot(normed_one, weights[0], preferred_element_type=jnp.float32),
        cosine_table,
        sine_table,
    ).astype(jnp.bfloat16)
    key_proj = rotate(
        jnp.dot(normed_one, weights[1], preferred_element_type=jnp.float32),
        cosine_table,
        sine_table,
    ).astype(jnp.bfloat16)
    value_proj = jnp.dot(normed_one, weights[2], preferred_element_type=jnp.float32).astype(
        jnp.bfloat16
    )
    key_values = jnp.concatenate([key_proj, value_proj], axis=1)
    segments_low = segment_ids.astype(jnp.bfloat16)
    gathered = gather_keys(key_values, segments_low)
    query_head_rows = queries.reshape(rows_here, KV_HEADS, repeat, HEAD)
    log_total, attention_output = attend_forward(
        query_head_rows, gathered, segments_low, query_index, logit_scale
    )
    attended_low = attention_output.reshape(rows_here, HEADS * HEAD).astype(jnp.bfloat16)
    middle = hidden + jnp.dot(attended_low, weights[3], preferred_element_type=jnp.float32)
    inverse_two = lax.rsqrt(jnp.mean(middle * middle, axis=1, keepdims=True) + EPSILON)
    normed_two = (middle * inverse_two * gain_two).astype(jnp.bfloat16)
    gate_out = jnp.dot(normed_two, weights[4], preferred_element_type=jnp.float32)
    up_out = jnp.dot(normed_two, weights[5], preferred_element_type=jnp.float32)
    inner_act = (jax.nn.silu(gate_out) * up_out).astype(jnp.bfloat16)
    mixed_out = (
        middle + jnp.dot(inner_act, weights[6], preferred_element_type=jnp.float32)
    ).astype(jnp.bfloat16)
    weights, gain_rows = gather_weights(shards, norm_gains)
    gathered = gather_keys(key_values, segments_low)
    down_weight_grad = jnp.einsum(
        "tf,td->fd", inner_act, cotangent, preferred_element_type=jnp.float32
    )
    inner_grad = jnp.einsum("td,fd->tf", cotangent, weights[6], preferred_element_type=jnp.float32)
    sigmoid_gate = jax.nn.sigmoid(gate_out)
    silu_gate = gate_out * sigmoid_gate
    gate_grad_low = (
        inner_grad * up_out * sigmoid_gate * (1.0 + gate_out * (1.0 - sigmoid_gate))
    ).astype(jnp.bfloat16)
    up_grad_low = (inner_grad * silu_gate).astype(jnp.bfloat16)
    gate_weight_grad = jnp.einsum(
        "td,tf->df", normed_two, gate_grad_low, preferred_element_type=jnp.float32
    )
    up_weight_grad = jnp.einsum(
        "td,tf->df", normed_two, up_grad_low, preferred_element_type=jnp.float32
    )
    normed_two_grad = jnp.einsum(
        "tf,df->td", gate_grad_low, weights[4], preferred_element_type=jnp.float32
    )
    normed_two_grad = normed_two_grad + jnp.einsum(
        "tf,df->td", up_grad_low, weights[5], preferred_element_type=jnp.float32
    )
    middle_grad, gain_two_grad = norm_back(middle, inverse_two, gain_two, normed_two_grad)
    middle_grad = middle_grad + cotangent.astype(jnp.float32)
    branch_low = middle_grad.astype(jnp.bfloat16)
    out_weight_grad = jnp.einsum(
        "tc,td->cd", attended_low, branch_low, preferred_element_type=jnp.float32
    )
    attention_output_grad = jnp.einsum(
        "td,cd->tc", branch_low, weights[3], preferred_element_type=jnp.float32
    ).astype(jnp.bfloat16)
    query_part, key_value_part = attend_backward(
        query_head_rows,
        gathered,
        segments_low,
        query_index,
        logit_scale,
        log_total,
        attention_output,
        attention_output_grad.reshape(rows_here, KV_HEADS, repeat, HEAD),
    )
    own_grads = lax.psum_scatter(key_value_part, "ctx", scatter_dimension=0, tiled=True)
    query_low = rotate(
        query_part.reshape(rows_here, HEADS * HEAD) * logit_scale, cosine_table, -sine_table
    ).astype(jnp.bfloat16)
    key_low = rotate(own_grads[:, :key_width] * logit_scale, cosine_table, -sine_table).astype(
        jnp.bfloat16
    )
    value_low = own_grads[:, key_width:].astype(jnp.bfloat16)
    query_weight_grad = jnp.einsum(
        "td,tc->dc", normed_one, query_low, preferred_element_type=jnp.float32
    )
    key_weight_grad = jnp.einsum(
        "td,tc->dc", normed_one, key_low, preferred_element_type=jnp.float32
    )
    value_weight_grad = jnp.einsum(
        "td,tc->dc", normed_one, value_low, preferred_element_type=jnp.float32
    )
    normed_one_grad = jnp.einsum(
        "tc,dc->td", query_low, weights[0], preferred_element_type=jnp.float32
    )
    normed_one_grad = normed_one_grad + jnp.einsum(
        "tc,dc->td", key_low, weights[1], preferred_element_type=jnp.float32
    )
    normed_one_grad = normed_one_grad + jnp.einsum(
        "tc,dc->td", value_low, weights[2], preferred_element_type=jnp.float32
    )
    hidden_grad, gain_one_grad = norm_back(hidden, inverse_one, gain_one, normed_one_grad)
    token_grad = middle_grad + hidden_grad
    gain_terms = jnp.stack([gain_one_grad, gain_two_grad])
    reduced = (
        lax.psum_scatter(query_weight_grad, "ctx", scatter_dimension=0, tiled=True),
        lax.psum_scatter(key_weight_grad, "ctx", scatter_dimension=0, tiled=True),
        lax.psum_scatter(value_weight_grad, "ctx", scatter_dimension=0, tiled=True),
        lax.psum_scatter(out_weight_grad, "ctx", scatter_dimension=0, tiled=True),
        lax.psum_scatter(gate_weight_grad, "ctx", scatter_dimension=0, tiled=True),
        lax.psum_scatter(up_weight_grad, "ctx", scatter_dimension=0, tiled=True),
        lax.psum_scatter(down_weight_grad, "ctx", scatter_dimension=0, tiled=True),
        lax.psum_scatter(gain_terms, "ctx", scatter_dimension=1, tiled=True),
    )
    copies = jnp.tile(reduced[7], (1, lax.axis_size("dp")))
    owned_grads = (
        lax.psum_scatter(
            reduced[0].astype(jnp.bfloat16), "dp", scatter_dimension=1, tiled=True
        ).astype(jnp.float32),
        lax.psum_scatter(
            reduced[1].astype(jnp.bfloat16), "dp", scatter_dimension=1, tiled=True
        ).astype(jnp.float32),
        lax.psum_scatter(
            reduced[2].astype(jnp.bfloat16), "dp", scatter_dimension=1, tiled=True
        ).astype(jnp.float32),
        lax.psum_scatter(
            reduced[3].astype(jnp.bfloat16), "dp", scatter_dimension=1, tiled=True
        ).astype(jnp.float32),
        lax.psum_scatter(
            reduced[4].astype(jnp.bfloat16), "dp", scatter_dimension=1, tiled=True
        ).astype(jnp.float32),
        lax.psum_scatter(
            reduced[5].astype(jnp.bfloat16), "dp", scatter_dimension=1, tiled=True
        ).astype(jnp.float32),
        lax.psum_scatter(
            reduced[6].astype(jnp.bfloat16), "dp", scatter_dimension=1, tiled=True
        ).astype(jnp.float32),
        lax.psum_scatter(copies.astype(jnp.bfloat16), "dp", scatter_dimension=1, tiled=True).astype(
            jnp.float32
        ),
    )
    return (
        mixed_out,
        token_grad,
        owned_grads[7],
        owned_grads[0],
        owned_grads[1],
        owned_grads[2],
        owned_grads[3],
        owned_grads[4],
        owned_grads[5],
        owned_grads[6],
    )


def z_permute(block, shift, wrap):
    size = lax.axis_size("ctx")
    pairs = [
        (c, (c + 2 * shift) % size)
        for c in range(size)
        if wrap or 0 <= c + 2 * shift < size
    ]
    return lax.ppermute(block, "ctx", pairs)


def core_permute(block):
    return lax.ppermute(block, "ctx", [(c, c ^ 1) for c in range(lax.axis_size("ctx"))])


def dp_permute(block, offset):
    size = lax.axis_size("dp")
    return lax.ppermute(block, "dp", [(d, d ^ offset) for d in range(size)])


def place(pieces, indices):
    stacked = jnp.zeros((len(pieces),) + pieces[0].shape, pieces[0].dtype)
    for piece, index in zip(pieces, indices):
        stacked = lax.dynamic_update_index_in_dim(stacked, piece, index, 0)
    return stacked


def core_pair(mine, other):
    first = lax.axis_index("ctx") % 2 == 0
    return (jnp.where(first, mine, other), jnp.where(first, other, mine))


def gather_z(block):
    depth = lax.axis_size("ctx") // 2
    level = lax.axis_index("ctx") // 2
    return place(
        [block] + [z_permute(block, s, True) for s in range(1, depth)],
        [(level - s) % depth for s in range(depth)],
    )


def gather_dp(along):
    column = lax.axis_index("dp")
    size = lax.axis_size("dp")
    pieces = [along] + [dp_permute(along, s) for s in range(1, size)]
    for bit in (1, 2):
        swapped = column & bit != 0
        pieces = [jnp.where(swapped, pieces[n ^ bit], pieces[n]) for n in range(size)]
    return jnp.stack(pieces)


def gather_core(across):
    even, odd = core_pair(across, core_permute(across))
    both = jnp.stack([even, odd], axis=2)
    dp, depth, cores, rows, width = both.shape
    return both.reshape(dp, depth * cores * rows, width)


def sum_core(blocks):
    depth = lax.axis_size("ctx") // 2
    core = lax.axis_index("ctx") % 2
    dp, rows, width = blocks.shape
    blocks = blocks.reshape(dp, depth, 2, rows // (2 * depth), width)
    kept = lax.dynamic_index_in_dim(blocks, core, 2, keepdims=False)
    sent = lax.dynamic_index_in_dim(blocks, 1 - core, 2, keepdims=False)
    return (kept.astype(jnp.float32) + core_permute(sent).astype(jnp.float32)).astype(jnp.bfloat16)


def sum_dp(half):
    column = lax.axis_index("dp")
    total = lax.dynamic_index_in_dim(half, column, 0, keepdims=False).astype(jnp.float32)
    for s in range(1, lax.axis_size("dp")):
        part = lax.dynamic_index_in_dim(half, column ^ s, 0, keepdims=False)
        total = total + dp_permute(part, s).astype(jnp.float32)
    return total.astype(jnp.bfloat16)


def sum_z(quarter):
    depth = lax.axis_size("ctx") // 2
    level = lax.axis_index("ctx") // 2
    result = lax.dynamic_index_in_dim(quarter, level, 0, keepdims=False).astype(jnp.float32)
    for s in range(1, depth):
        part = lax.dynamic_index_in_dim(quarter, (level + s) % depth, 0, keepdims=False)
        result = result + z_permute(part, s, True).astype(jnp.float32)
    return result


def dot_nt(left, right):
    return lax.dot_general(left, right, (((1,), (1,)), ((), ())), preferred_element_type=jnp.float32)


def dot_tn(left, right):
    return lax.dot_general(left, right, (((0,), (0,)), ((), ())), preferred_element_type=jnp.float32)


def dot_nn(left, right):
    return jnp.dot(left, right, preferred_element_type=jnp.float32)


def kept_pairs(row_ref, key_segment_ref):
    rows, length = row_ref.shape[0], key_segment_ref.shape[1]
    key_index = lax.broadcasted_iota(jnp.int32, (rows, length), 1)
    return (row_ref[:, 1:2] == key_segment_ref[...]) & (key_index <= row_ref[:, 0:1])


def forward_kernel(q_ref, kv_ref, row_ref, key_segment_ref, out_ref, lse_ref):
    keep = kept_pairs(row_ref, key_segment_ref)
    outputs = []
    for i in range(HEADS):
        j = i // (HEADS // KV_HEADS)
        key = kv_ref[:, j * HEAD : (j + 1) * HEAD]
        value = kv_ref[:, (KV_HEADS + j) * HEAD : (KV_HEADS + j + 1) * HEAD]
        scores = dot_nt(q_ref[:, i * HEAD : (i + 1) * HEAD], key) * HEAD ** (-0.5)
        scores = jnp.where(keep, scores, MASKED)
        top = jnp.max(scores, axis=1, keepdims=True)
        total = jnp.sum(jnp.exp(scores - top), axis=1, keepdims=True)
        log_total = top + jnp.log(total)
        lse_ref[i] = log_total
        outputs.append(dot_nn(jnp.exp(scores - log_total).astype(jnp.bfloat16), value))
    out_ref[...] = jnp.concatenate(outputs, axis=1)


def backward_kernel(
    q_ref, kv_ref, row_ref, key_segment_ref, lse_ref, out_ref, grad_ref, dq_ref, dkv_ref
):
    keep = kept_pairs(row_ref, key_segment_ref)
    query_parts, key_parts, value_parts = [], [], []
    repeat = HEADS // KV_HEADS
    for j in range(KV_HEADS):
        key = kv_ref[:, j * HEAD : (j + 1) * HEAD]
        value = kv_ref[:, (KV_HEADS + j) * HEAD : (KV_HEADS + j + 1) * HEAD]
        key_part = value_part = None
        for i in range(j * repeat, (j + 1) * repeat):
            query = q_ref[:, i * HEAD : (i + 1) * HEAD]
            grad = grad_ref[:, i * HEAD : (i + 1) * HEAD]
            out = out_ref[:, i * HEAD : (i + 1) * HEAD]
            delta = jnp.sum(grad.astype(jnp.float32) * out, axis=1, keepdims=True)
            scores = jnp.where(keep, dot_nt(query, key) * HEAD ** (-0.5), MASKED)
            weight = jnp.exp(scores - lse_ref[i])
            slope = (weight * (dot_nt(grad, value) - delta)).astype(jnp.bfloat16)
            query_parts.append(dot_nn(slope, key))
            dk = dot_tn(slope, query)
            dv = dot_tn(weight.astype(jnp.bfloat16), grad)
            key_part = dk if key_part is None else key_part + dk
            value_part = dv if value_part is None else value_part + dv
        key_parts.append(key_part)
        value_parts.append(value_part)
    dq_ref[...] = jnp.concatenate(query_parts, axis=1)
    dkv_ref[...] = jnp.concatenate(key_parts + value_parts, axis=1)


def run_kernel(kernel, operands, shapes, flops):
    return pl.pallas_call(
        kernel,
        out_shape=[jax.ShapeDtypeStruct(shape, jnp.float32) for shape in shapes],
        in_specs=[pl.BlockSpec(memory_space=pltpu.VMEM)] * len(operands),
        out_specs=[pl.BlockSpec(memory_space=pltpu.VMEM)] * len(shapes),
        compiler_params=pltpu.CompilerParams(vmem_limit_bytes=48 * 1024 * 1024),
        cost_estimate=pl.CostEstimate(
            flops=flops, bytes_accessed=8 * 1024 * 1024, transcendentals=10 * 1024 * 1024
        ),
    )(*operands)


def chain_gather(block):
    depth = lax.axis_size("ctx") // 2
    level = lax.axis_index("ctx") // 2
    along = place(
        [block] + [z_permute(block, s, False) for s in range(1, depth)],
        [(level - s) % depth for s in range(depth)],
    )
    even, odd = core_pair(along, core_permute(along))
    return jnp.stack([even, odd], axis=1)


def chain_sum(blocks):
    depth = lax.axis_size("ctx") // 2
    level = lax.axis_index("ctx") // 2
    core = lax.axis_index("ctx") % 2
    kept = lax.dynamic_index_in_dim(blocks, core, 1, keepdims=False)
    sent = lax.dynamic_index_in_dim(blocks, 1 - core, 1, keepdims=False).astype(jnp.bfloat16)
    half = kept + core_permute(sent).astype(jnp.float32)
    result = lax.dynamic_index_in_dim(half, level, 0, keepdims=False)
    for s in range(1, depth):
        part = lax.dynamic_index_in_dim(half, (level - s) % depth, 0, keepdims=False)
        result = result + z_permute(part.astype(jnp.bfloat16), -s, False).astype(jnp.float32)
    return result


def staged_body(
    tokens,
    segment_ids,
    positions,
    norm_gains,
    w_query,
    w_key,
    w_value,
    w_out,
    w_gate,
    w_up,
    w_down,
    cotangent,
):
    f32, bf16 = jnp.float32, jnp.bfloat16
    nq, nk, ng = w_query.shape[1], w_key.shape[1], w_gate.shape[1]
    dp = lax.axis_size("dp")
    ctx = lax.axis_size("ctx")
    rows = tokens.shape[0]
    key_width = KV_HEADS * HEAD
    logit_scale = HEAD ** (-0.5)
    first = gather_z(jnp.concatenate([w_query, w_key, w_value, norm_gains.T], axis=1))
    early, late = lax.optimization_barrier(
        (first, (jnp.concatenate([w_gate, w_up, w_out], axis=1), w_down))
    )
    first = gather_core(gather_dp(early))
    second, third = gather_z(late[0]), gather_z(late[1])

    def wide(begin, width):
        return jnp.transpose(first[..., begin : begin + width], (1, 0, 2)).reshape(-1, dp * width)

    wq, wk, wv = wide(0, nq), wide(nq, nk), wide(nq + nk, nk)
    gain_rows = first[0, :, nq + 2 * nk :].T.astype(f32)
    gain_one, gain_two = gain_rows[0], gain_rows[1]
    cosine_table, sine_table = tables(positions)
    hidden = tokens.astype(f32)
    inverse_one = lax.rsqrt(jnp.mean(hidden * hidden, axis=1, keepdims=True) + EPSILON)
    normed_one = (hidden * inverse_one * gain_one).astype(bf16)
    key_proj = rotate(dot_nn(normed_one, wk), cosine_table, sine_table).astype(bf16)
    value_proj = dot_nn(normed_one, wv).astype(bf16)
    spare = jnp.zeros((16, 2 * key_width), bf16).at[0, :rows].set(segment_ids.astype(bf16))
    sent = jnp.concatenate([jnp.concatenate([key_proj, value_proj], axis=1), spare], axis=0)
    sent, second, third = lax.optimization_barrier((sent, second, third))
    second, third = gather_dp(second), gather_dp(third)
    queries = rotate(dot_nn(normed_one, wq), cosine_table, sine_table).astype(bf16)
    parts = chain_gather(sent)
    parts, second, third = lax.optimization_barrier((parts, second, third))
    key_values = parts[:, :, :rows].reshape(-1, 2 * key_width)
    key_segments = parts[:, :, rows, :rows].reshape(1, -1).astype(jnp.int32)
    query_index = lax.axis_index("ctx") * rows + jnp.arange(rows, dtype=jnp.int32)
    row_facts = jnp.stack([query_index, segment_ids], axis=1)
    length = key_values.shape[0]
    shared = (queries, key_values, row_facts, key_segments)
    pair_flops = 2 * HEADS * HEAD * rows * length
    attention_output, log_total = run_kernel(
        forward_kernel, shared, [(rows, HEADS * HEAD), (HEADS, rows, 1)], 2 * pair_flops
    )
    second, third = gather_core(second), gather_core(third)
    wg, wo = second[..., : 2 * ng], second[..., 2 * ng :]

    def lanes(blocks):
        return jnp.concatenate([blocks[n] for n in range(dp)], axis=1)

    def apart(matrix):
        width = matrix.shape[1] // dp
        return jnp.stack([matrix[:, n * width : (n + 1) * width] for n in range(dp)])

    def forth(matrix, blocks):
        return jnp.einsum("tk,dkn->dtn", matrix, blocks, preferred_element_type=f32)

    def back(parts_in, blocks):
        return sum(dot_nt(parts_in[n], blocks[n]) for n in range(dp))

    def grads(matrix, parts_in):
        return jnp.stack([dot_tn(matrix, parts_in[n]).astype(bf16) for n in range(dp)])

    attended_low = attention_output.astype(bf16)
    middle = hidden + lanes(forth(attended_low, wo))
    inverse_two = lax.rsqrt(jnp.mean(middle * middle, axis=1, keepdims=True) + EPSILON)
    normed_two = (middle * inverse_two * gain_two).astype(bf16)
    gate_up = forth(normed_two, wg)
    gate_out, up_out = gate_up[..., :ng], gate_up[..., ng:]
    sigmoid_gate = jax.nn.sigmoid(gate_out)
    silu_gate = gate_out * sigmoid_gate
    inner_act = lanes((silu_gate * up_out).astype(bf16))
    mixed_out = (middle + lanes(forth(inner_act, third))).astype(bf16)
    upstream = apart(cotangent)
    down_half = sum_core(grads(inner_act, upstream))
    inner_grad = apart(back(upstream, third))
    gate_low = inner_grad * up_out * sigmoid_gate * (1.0 + gate_out * (1.0 - sigmoid_gate))
    slopes = jnp.concatenate([gate_low.astype(bf16), (inner_grad * silu_gate).astype(bf16)], axis=2)
    gate_half = sum_core(grads(normed_two, slopes))
    middle_grad, gain_two_grad = norm_back(middle, inverse_two, gain_two, back(slopes, wg))
    middle_grad = middle_grad + cotangent.astype(f32)
    branch = apart(middle_grad.astype(bf16))
    attention_grad = back(branch, wo).astype(bf16)
    out_half = sum_core(grads(attended_low, branch))
    attention_grad, down_half, gate_half = lax.optimization_barrier(
        (attention_grad, down_half, gate_half)
    )
    query_part, key_value_part = run_kernel(
        backward_kernel,
        shared + (log_total, attention_output, attention_grad),
        [(rows, HEADS * HEAD), (length, 2 * key_width)],
        5 * pair_flops,
    )
    down_part, gate_part, out_part = sum_dp(down_half), sum_dp(gate_half), sum_dp(out_half)
    own_grads = chain_sum(key_value_part.reshape(ctx // 2, 2, rows, 2 * key_width))
    query_low = rotate(query_part * logit_scale, cosine_table, -sine_table).astype(bf16)
    own_grads, down_part, gate_part, out_part = lax.optimization_barrier(
        (own_grads, down_part, gate_part, out_part)
    )
    key_low = rotate(own_grads[:, :key_width] * logit_scale, cosine_table, -sine_table)
    key_low = key_low.astype(bf16)
    value_low = own_grads[:, key_width:].astype(bf16)
    normed_one_grad = dot_nt(query_low, wq) + dot_nt(key_low, wk) + dot_nt(value_low, wv)
    hidden_grad, gain_one_grad = norm_back(hidden, inverse_one, gain_one, normed_one_grad)
    token_grad = middle_grad + hidden_grad
    gain_terms = jnp.stack([gain_one_grad, gain_two_grad], axis=1).astype(bf16)
    joined = jnp.concatenate([apart(query_low), apart(key_low), apart(value_low)], axis=2)
    gain_blocks = jnp.broadcast_to(gain_terms[None], (dp,) + gain_terms.shape)
    first_grad = jnp.concatenate([grads(normed_one, joined), gain_blocks], axis=2)
    first_grad = sum_z(sum_dp(sum_core(first_grad)))
    down_grad, gate_grad, out_grad = sum_z(down_part), sum_z(gate_part), sum_z(out_part)
    return (
        mixed_out,
        token_grad,
        first_grad[:, nq + 2 * nk :].T,
        first_grad[:, :nq],
        first_grad[:, nq : nq + nk],
        first_grad[:, nq + nk : nq + 2 * nk],
        out_grad,
        gate_grad[:, :ng],
        gate_grad[:, ng:],
        down_grad,
    )


def solution(mesh):
    dp, ctx = mesh.shape["dp"], mesh.shape["ctx"]
    placed = (
        P(("dp", "ctx"), None),
        P(("dp", "ctx")),
        P(("dp", "ctx")),
        P(None, "ctx"),
        P("ctx", "dp"),
        P("ctx", "dp"),
        P("ctx", "dp"),
        P("ctx", "dp"),
        P("ctx", "dp"),
        P("ctx", "dp"),
        P("ctx", "dp"),
        P(("dp", "ctx"), None),
    )
    return jax.shard_map(
        staged_body if dp == 4 and ctx == 8 else body,
        mesh=mesh,
        in_specs=placed,
        out_specs=(
            P(("dp", "ctx"), None),
            P(("dp", "ctx"), None),
            P(None, "ctx"),
            P("ctx", "dp"),
            P("ctx", "dp"),
            P("ctx", "dp"),
            P("ctx", "dp"),
            P("ctx", "dp"),
            P("ctx", "dp"),
            P("ctx", "dp"),
        ),
        check_vma=False,
    )
```
